32 devices in a mesh: batch: 2 (over x), seq: 16 (over z, y, core).
Axes of the slice: x: 2, y: 2, z: 4, core: 2. Of those that a mesh axis runs over, the one named last changes fastest.
Arguments:
- signal: bfloat16 [2, 262144, 384], P('batch', 'seq'), may hold values from -6 to 6
- conv_weight: float32 [4, 384], replicated, may hold values from -2.5 to 2.5
- first_factor: bfloat16 [512, 512, 512], P('seq'), may hold values from -0.25 to 0.25
- second_factor: bfloat16 [512, 512, 512], P('seq'), may hold values from -0.25 to 0.25
- grad_output: bfloat16 [2, 262144, 384], P('batch', 'seq'), may hold values from -3 to 3
Outputs:
- grad_signal: bfloat16 [2, 262144, 384], P('batch', 'seq')
- grad_first: bfloat16 [512, 512, 512], P('seq', 'batch')
- grad_second: bfloat16 [512, 512, 512], P('seq', 'batch')
The draws below stay inside these ranges and needn't reach their ends.
All inputs are finite; a program needn't handle non-finite values.
Results may differ from the reference program's by a relative error of at most 0.0065.
Values may be sent and summed in bfloat16 or wider, within the bound.
No kernel may reach another device: no remote copies, remote signals or barrier semaphores. Data moves between devices by JAX's collectives and lax.ppermute only.
A program may use at most 320 MiB of HBM per device.

```python
import jax
import jax.numpy as jnp
from jax import lax

D = 384
NB = 512
BS = 512
KW = 4
SEQ_DEV = 1
L = 262144
NSEQ = 2
N_BATCH = 2


def block_levels(own_key, dims, shards, least, top_value):
    factor_of, own = 1.0, jax.random.fold_in(own_key, 6)
    for dim, parts in shards:
        steps = jnp.exp(jax.random.uniform(jax.random.fold_in(own, dim), (parts,), jnp.float32, least / len(shards), top_value / len(shards)))
        factor_of = factor_of * jnp.repeat(steps, dims[dim] // parts).reshape([-1 if axis == dim else 1 for axis in range(len(dims))])
    return factor_of


def centred(stream_key, extent, width, bound, shards=(), held_as=jnp.bfloat16):
    gain = block_levels(stream_key, extent, shards, -0.22, 0.18) if shards else 1.0
    entries = jax.random.normal(stream_key, extent, jnp.float32) * width * gain
    return jnp.minimum(jnp.maximum(entries, -bound), bound).astype(held_as)


def setup_inputs(seed: int = 0) -> dict:
    arg_keys = jax.random.split(jax.random.key(seed), 6)
    return {
        "signal": centred(arg_keys[0], (NSEQ, L, D), 1.0, 6.0, ((0, 2), (1, 16))),
        "conv_weight": centred(arg_keys[1], (KW, D), 0.5, 2.5, (), jnp.float32),
        "first_factor": centred(arg_keys[2], (NB, BS, BS), BS ** -0.5, 0.25, ((0, 16),)),
        "second_factor": centred(arg_keys[3], (BS, NB, NB), NB ** -0.5, 0.25, ((0, 16),)),
        "grad_output": centred(arg_keys[4], (NSEQ, L, D), 0.5, 3.0, ((0, 2), (1, 16))),
    }


def reference(signal, conv_weight, first_factor, second_factor, grad_output):
    seq_count = signal.shape[0]
    signal_f = signal.astype(jnp.float32)
    padded_in = jnp.pad(signal_f, ((0, 0), (KW - 1, 0), (0, 0)))
    conv_out = sum(conv_weight[r][None, None, :] * padded_in[:, KW - 1 - r:KW - 1 - r + L, :] for r in range(KW))
    gate_val = jax.nn.sigmoid(conv_out)
    hidden = (conv_out * gate_val).astype(jnp.bfloat16)
    hidden_blocks = hidden.reshape(seq_count, NB, BS, D)
    first_f = first_factor.astype(jnp.float32)
    second_f = second_factor.astype(jnp.float32)
    mixed = jnp.einsum('ikj,sijd->sikd', first_f, hidden_blocks.astype(jnp.float32)).astype(jnp.bfloat16)
    upstream = grad_output.reshape(seq_count, BS, NB, D)
    grad_mixed = jnp.einsum('kmi,skmd->sikd', second_f, upstream.astype(jnp.float32)).astype(jnp.bfloat16)
    grad_hidden = jnp.einsum('ikj,sikd->sijd', first_f, grad_mixed.astype(jnp.float32)).reshape(seq_count, L, D)
    grad_conv = (grad_hidden * gate_val * (1.0 + conv_out * (1.0 - gate_val))).astype(jnp.bfloat16)
    padded_back = jnp.pad(grad_conv.astype(jnp.float32), ((0, 0), (0, KW - 1), (0, 0)))
    grad_signal = sum(conv_weight[r][None, None, :] * padded_back[:, r:r + L, :] for r in range(KW)).astype(jnp.bfloat16)
    total_first = jnp.zeros((NB, BS, BS), jnp.float32)
    total_second = jnp.zeros((BS, NB, NB), jnp.float32)
    for group in range(N_BATCH):
        low = group * SEQ_DEV
        part_mixed = grad_mixed[low:low + SEQ_DEV].astype(jnp.float32)
        part_hidden = hidden_blocks[low:low + SEQ_DEV].astype(jnp.float32)
        part_up = upstream[low:low + SEQ_DEV].astype(jnp.float32)
        part_fwd = mixed[low:low + SEQ_DEV].astype(jnp.float32)
        part_first = jnp.einsum('sikd,sijd->ikj', part_mixed, part_hidden).astype(jnp.bfloat16)
        part_second = jnp.einsum('skmd,sikd->kmi', part_up, part_fwd).astype(jnp.bfloat16)
        total_first = total_first + lax.optimization_barrier(part_first).astype(jnp.float32)
        total_second = total_second + lax.optimization_barrier(part_second).astype(jnp.float32)
    return grad_signal, total_first.astype(jnp.bfloat16), total_second.astype(jnp.bfloat16)
```

```python
import functools

import jax
import jax.numpy as jnp
from jax import lax
from jax.experimental import pallas as pl
from jax.experimental.pallas import tpu as pltpu
from jax.sharding import PartitionSpec as P

ROW_TILE = 16
VMEM = 48 * 2**20
WEIGHT = 1


def passed_along(value, axis, steps):
    count = lax.axis_size(axis)
    initial, last = (max(0, -steps), min(count, count - steps))
    return lax.ppermute(value, axis, [(source, source + steps) for source in range(initial, last)])


def cuts(total, sizes):
    if sum(sizes) != total:
        sizes = (total,)
    return [(sum(sizes[:n]), size) for n, size in enumerate(sizes)]


def split_product_kernel(factor_ref, rows_ref, *out_refs):
    product = lax.dot_general(
        factor_ref[0], rows_ref[0], (((0,), (0,)), ((), ())), preferred_element_type=jnp.float32
    ).astype(jnp.bfloat16)
    devices = out_refs[0].shape[0]
    per_device = product.shape[0] // devices
    start = 0
    dealt = product.reshape(devices, per_device, product.shape[1])
    for out_ref in out_refs:
        size = out_ref.shape[2]
        out_ref[:, 0] = dealt[:, start : start + size]
        start += size


def split_product(factor, rows, devices, pieces):
    blocks, depth, width = factor.shape
    channels = rows.shape[2]
    if any(size % ROW_TILE for _, size in pieces):
        product = jnp.einsum("kmi,kmd->kid", factor, rows, preferred_element_type=jnp.float32)
        product = product.astype(jnp.bfloat16).reshape(blocks, devices, width // devices, channels)
        return [
            product[:, :, start : start + size].transpose(1, 0, 2, 3) for start, size in pieces
        ]
    return pl.pallas_call(
        split_product_kernel,
        grid=(blocks,),
        in_specs=[
            pl.BlockSpec((1, depth, width), lambda k: (k, 0, 0)),
            pl.BlockSpec((1, depth, channels), lambda k: (k, 0, 0)),
        ],
        out_specs=[
            pl.BlockSpec((devices, 1, size, channels), lambda k: (0, k, 0, 0)) for _, size in pieces
        ],
        out_shape=[
            jax.ShapeDtypeStruct((devices, blocks, size, channels), jnp.bfloat16) for _, size in pieces
        ],
        compiler_params=pltpu.CompilerParams(vmem_limit_bytes=VMEM),
        cost_estimate=pl.CostEstimate(
            flops=2 * blocks * depth * width * channels,
            bytes_accessed=2 * blocks * (depth * width + depth * channels + width * channels),
            transcendentals=0,
        ),
    )(factor, rows)


def outer_kernel(left_ref, right_ref, out_ref):
    left, right = left_ref[...], right_ref[...]
    channels = left.shape[-1]
    product = lax.dot_general(
        left.reshape(-1, channels),
        right.reshape(-1, channels),
        (((1,), (1,)), ((), ())),
        preferred_element_type=jnp.float32,
    ).astype(jnp.bfloat16)
    out_ref[:, 0] = product.reshape(out_ref.shape[0], -1, product.shape[1])


def outer(left, right, halves, start=0, right_start=0):
    channels = left.shape[2]
    rows = left.shape[1]
    if right.ndim == 4:
        devices, blocks, part, _ = right.shape
        cols = devices * part
        if part % ROW_TILE:
            right = right.transpose(1, 0, 2, 3).reshape(blocks, cols, channels)
            right_spec = pl.BlockSpec((1, cols, channels), lambda b: (b, 0, 0))
        else:
            right_spec = pl.BlockSpec((devices, 1, part, channels), lambda b: (0, b, 0, 0))
    else:
        cols = right.shape[1]
        blocks = left.shape[0]
        right_spec = pl.BlockSpec((1, cols, channels), lambda b: (b + right_start, 0, 0))
    return pl.pallas_call(
        outer_kernel,
        grid=(blocks,),
        in_specs=[pl.BlockSpec((1, rows, channels), lambda b: (b + start, 0, 0)), right_spec],
        out_specs=pl.BlockSpec((halves, 1, rows // halves, cols), lambda b: (0, b, 0, 0)),
        out_shape=jax.ShapeDtypeStruct((halves, blocks, rows // halves, cols), jnp.bfloat16),
        compiler_params=pltpu.CompilerParams(vmem_limit_bytes=VMEM),
        cost_estimate=pl.CostEstimate(
            flops=2 * blocks * rows * cols * channels,
            bytes_accessed=2 * blocks * (rows * cols + rows * channels + cols * channels),
            transcendentals=0,
        ),
    )(left, right)


def back_kernel(factor_ref, rows_ref, slope_ref, out_ref):
    product = lax.dot_general(
        factor_ref[0], rows_ref[0], (((0,), (0,)), ((), ())), preferred_element_type=jnp.float32
    )
    out_ref[...] = (product * slope_ref[...]).astype(jnp.bfloat16)


def back(factor, rows, slope, start):
    blocks, depth, channels = rows.shape
    width = factor.shape[2]
    return pl.pallas_call(
        back_kernel,
        grid=(blocks,),
        in_specs=[
            pl.BlockSpec((1, depth, width), lambda b: (b + start, 0, 0)),
            pl.BlockSpec((1, depth, channels), lambda b: (b, 0, 0)),
            pl.BlockSpec((width, channels), lambda b: (b + start, 0)),
        ],
        out_specs=pl.BlockSpec((width, channels), lambda b: (b, 0)),
        out_shape=jax.ShapeDtypeStruct((blocks * width, channels), jnp.bfloat16),
        compiler_params=pltpu.CompilerParams(vmem_limit_bytes=VMEM),
        cost_estimate=pl.CostEstimate(
            flops=WEIGHT * 2 * blocks * depth * width * channels,
            bytes_accessed=WEIGHT * 2 * blocks * (depth * width + depth * channels + 3 * width * channels),
            transcendentals=0,
        ),
    )(factor, rows, slope)


def signal_kernel(cuts_, taps, *refs):
    pieces, firsts = refs[: len(cuts_)], refs[len(cuts_) : 2 * len(cuts_)]
    following_ref, weight_ref, out_ref = refs[2 * len(cuts_) :]
    block, last = pl.program_id(0), pl.num_programs(0) - 1

    def spread(rows, next_rows):
        rows = rows[...].astype(jnp.float32)
        extended = jnp.concatenate([rows, next_rows[...].astype(jnp.float32)], axis=0)
        total = weight_ref[0:1, :] * rows
        for r in range(1, taps):
            ahead = pltpu.roll(extended, extended.shape[0] - r, 0)[: rows.shape[0]]
            total += weight_ref[r : r + 1, :] * ahead
        out_ref[...] = total.astype(jnp.bfloat16)

    for n, (start, size) in enumerate(cuts_):
        end = start + size - 1

        @pl.when((block >= start) & (block < end))
        def _():
            spread(pieces[n], firsts[n])

        @pl.when(block == end)
        def _():
            spread(pieces[n], following_ref if n == len(cuts_) - 1 else firsts[n + 1])


def signal_back(grad_conv, following, conv_weight, cuts_, rows):
    channels = conv_weight.shape[1]
    blocks = sum(size for _, size in cuts_)
    following = jnp.pad(following, ((0, ROW_TILE - following.shape[0]), (0, 0)))
    step = rows // ROW_TILE

    def own(start, size):
        return lambda b: (jnp.clip(b - start, 0, size - 1), 0)

    def first_rows(start, size):
        return lambda b: (jnp.clip(b + 1 - start, 0, size - 1) * step, 0)

    return pl.pallas_call(
        functools.partial(signal_kernel, cuts_, conv_weight.shape[0]),
        grid=(blocks,),
        in_specs=[pl.BlockSpec((rows, channels), own(*cut)) for cut in cuts_]
        + [pl.BlockSpec((ROW_TILE, channels), first_rows(*cut)) for cut in cuts_]
        + [
            pl.BlockSpec((ROW_TILE, channels), lambda b: (0, 0)),
            pl.BlockSpec(conv_weight.shape, lambda b: (0, 0)),
        ],
        out_specs=pl.BlockSpec((rows, channels), lambda b: (b, 0)),
        out_shape=jax.ShapeDtypeStruct((blocks * rows, channels), jnp.bfloat16),
        compiler_params=pltpu.CompilerParams(vmem_limit_bytes=VMEM),
        cost_estimate=pl.CostEstimate(
            flops=WEIGHT * 8 * blocks * rows * channels,
            bytes_accessed=WEIGHT * 4 * blocks * rows * channels,
            transcendentals=0,
        ),
    )(*grad_conv, *grad_conv, following, conv_weight)


def summed_half(halves):
    return lax.psum_scatter(halves, "batch", scatter_dimension=0, tiled=False)


def body(signal, conv_weight, first_factor, second_factor, grad_output):
    _, tok_rows, channels = signal.shape
    blocks, block_order = first_factor.shape[0], first_factor.shape[1]
    col_blocks, block_count = second_factor.shape[0], second_factor.shape[1]
    tap_count = conv_weight.shape[0]
    devices, halves = lax.axis_size("seq"), lax.axis_size("batch")
    tail = tap_count - 1

    first_cuts = cuts(blocks, (16, 16))
    second_cuts = cuts(col_blocks, (20, 12))

    tied = lax.optimization_barrier

    def exchanged(sent):
        return lax.all_to_all(sent, "seq", 0, 0, tiled=True)

    def ordered(rows, size):
        return rows.reshape(block_order, size, channels).transpose(1, 0, 2)

    previous = passed_along(signal[0, tok_rows - tail :, :], "seq", 1)
    upstream = grad_output.reshape(col_blocks, block_count, channels)
    outgoing = split_product(second_factor, upstream, devices, first_cuts)
    *outgoing, previous = tied((*outgoing, previous))

    arrived = exchanged(outgoing[0])
    padded_in = jnp.concatenate([previous, signal[0]], axis=0).astype(jnp.float32)
    conv_out = sum(
        conv_weight[r][None, :] * padded_in[tail - r : tail - r + tok_rows, :] for r in range(tap_count)
    )
    gate_val = jax.nn.sigmoid(conv_out)
    hidden = (conv_out * gate_val).astype(jnp.bfloat16).reshape(blocks, block_order, channels)
    slope = gate_val * (1.0 + conv_out * (1.0 - gate_val))
    mixed = jnp.einsum(
        "ikj,ijd->ikd", first_factor, hidden, preferred_element_type=jnp.float32
    ).astype(jnp.bfloat16)
    by_owner = mixed.reshape(blocks, devices, col_blocks, channels).transpose(1, 2, 0, 3)
    pieces = [by_owner[:, start : start + size] for start, size in second_cuts]
    arrived, hidden, slope, *rest = tied((arrived, hidden, slope, *pieces, *outgoing[1:]))
    pieces, rest = rest[: len(pieces)], rest[len(pieces) :]

    halves_first, grad_conv = [], []
    for piece, sent in enumerate(rest):
        coming = exchanged(sent)
        rows = ordered(arrived, first_cuts[piece][1])
        halves_first.append(outer(rows, hidden, halves, right_start=first_cuts[piece][0]))
        grad_conv.append(back(first_factor, rows, slope, first_cuts[piece][0]))
        arrived, hidden, *pieces = tied((coming, hidden, *pieces, *grad_conv, *halves_first))
        grad_conv = pieces[len(second_cuts) : len(second_cuts) + piece + 1]
        del pieces[len(second_cuts) :]

    columns = exchanged(pieces[0])
    rows = ordered(arrived, first_cuts[-1][1])
    halves_first.append(outer(rows, hidden, halves, right_start=first_cuts[-1][0]))
    grad_conv.append(back(first_factor, rows, slope, first_cuts[-1][0]))
    following = passed_along(grad_conv[0][:tail, :], "seq", -1)
    grad_first = [summed_half(part) for part in halves_first]
    columns, following, part, grad_conv[-1], *pieces = tied(
        (columns, following, halves_first[-1], grad_conv[-1], *pieces[1:])
    )
    grad_signal = None

    grad_second = []
    for step, (start, size) in enumerate(second_cuts):
        coming = exchanged(pieces[step]) if pieces[step:] else None
        if step == len(second_cuts) - 2 or len(second_cuts) == 1:
            grad_signal = signal_back(grad_conv, following, conv_weight, first_cuts, block_order)
        part = outer(upstream, columns, halves, start=start)
        grad_second.append(summed_half(part))
        if coming is not None:
            columns, grad_signal, part, *rest = tied((coming, grad_signal, part, *pieces[step + 1 :]))
            pieces[step + 1 :] = rest
    return (
        grad_signal[None],
        jnp.concatenate(grad_first, axis=0),
        jnp.concatenate(grad_second, axis=0),
    )


def solution(mesh):
    placed = (
        P("batch", "seq", None),
        P(),
        P("seq", None, None),
        P("seq", None, None),
        P("batch", "seq", None),
    )
    return jax.shard_map(
        body,
        mesh=mesh,
        in_specs=placed,
        out_specs=(P("batch", "seq", None), P("seq", "batch", None), P("seq", "batch", None)),
        check_vma=False,
    )
```

```python
import functools

import jax
import jax.numpy as jnp
from jax import lax
from jax.experimental import pallas as pl
from jax.experimental.pallas import tpu as pltpu
from jax.sharding import PartitionSpec as P

ROW_TILE = 16
VMEM = 60 * 2**20
WEIGHT = 1


def passed_along(value, axis, steps):
    count = lax.axis_size(axis)
    initial, last = (max(0, -steps), min(count, count - steps))
    return lax.ppermute(value, axis, [(source, source + steps) for source in range(initial, last)])


def cuts(total, sizes):
    if sum(sizes) != total:
        sizes = (total,)
    return [(sum(sizes[:n]), size) for n, size in enumerate(sizes)]


def per_step(blocks, start=0):
    return next(n for n in (4, 2, 1) if blocks % n == 0 and start % n == 0)


def split_product_kernel(factor_ref, rows_ref, *out_refs):
    devices = out_refs[0].shape[0]
    for n in range(factor_ref.shape[0]):
        product = lax.dot_general(
            factor_ref[n], rows_ref[n], (((0,), (0,)), ((), ())), preferred_element_type=jnp.float32
        ).astype(jnp.bfloat16)
        dealt = product.reshape(devices, product.shape[0] // devices, product.shape[1])
        start = 0
        for out_ref in out_refs:
            size = out_ref.shape[2]
            out_ref[:, n] = dealt[:, start : start + size]
            start += size


def split_product(factor, rows, devices, pieces):
    blocks, depth, width = factor.shape
    channels = rows.shape[2]
    if any(size % ROW_TILE for _, size in pieces):
        product = jnp.einsum("kmi,kmd->kid", factor, rows, preferred_element_type=jnp.float32)
        product = product.astype(jnp.bfloat16).reshape(blocks, devices, width // devices, channels)
        return [
            product[:, :, start : start + size].transpose(1, 0, 2, 3) for start, size in pieces
        ]
    step = per_step(blocks)
    return pl.pallas_call(
        split_product_kernel,
        grid=(blocks // step,),
        in_specs=[
            pl.BlockSpec((step, depth, width), lambda k: (k, 0, 0)),
            pl.BlockSpec((step, depth, channels), lambda k: (k, 0, 0)),
        ],
        out_specs=[
            pl.BlockSpec((devices, step, size, channels), lambda k: (0, k, 0, 0)) for _, size in pieces
        ],
        out_shape=[
            jax.ShapeDtypeStruct((devices, blocks, size, channels), jnp.bfloat16) for _, size in pieces
        ],
        compiler_params=pltpu.CompilerParams(vmem_limit_bytes=VMEM),
        cost_estimate=pl.CostEstimate(
            flops=2 * blocks * depth * width * channels,
            bytes_accessed=2 * blocks * (depth * width + depth * channels + width * channels),
            transcendentals=0,
        ),
    )(factor, rows)


def outer_kernel(half_ref, left_ref, right_ref, *refs):
    out_ref = refs[-1]
    channels = left_ref.shape[-1]
    for n in range(left_ref.shape[0]):
        right = right_ref[n] if len(right_ref.shape) == 3 else right_ref[:, n].reshape(-1, channels)
        product = lax.dot_general(
            left_ref[n], right, (((1,), (1,)), ((), ())), preferred_element_type=jnp.float32
        ).astype(jnp.bfloat16)
        if len(refs) > 1:
            total = product.astype(jnp.float32) + refs[0][n].astype(jnp.float32)
            product = total.astype(jnp.bfloat16)
        out_ref[n] = product


def outer(half, left, right, start, received=None, into=None, total=None):
    halves = lax.axis_size("batch")
    rows, channels = left.shape[1] // halves, left.shape[2]
    if right.ndim == 4 and right.shape[2] % ROW_TILE:
        right = right.transpose(1, 0, 2, 3).reshape(right.shape[1], -1, channels)
    if right.ndim == 4:
        devices, blocks, part, _ = right.shape
        cols = devices * part
        step = per_step(blocks, start)
        right_spec = pl.BlockSpec((devices, step, part, channels), lambda b, h: (0, b, 0, 0))
        left_at, right_at = start // step, 0
    else:
        blocks, cols = min(left.shape[0], right.shape[0]), right.shape[1]
        step = per_step(blocks, start)
        left_at = start // step if left.shape[0] > blocks else 0
        right_at = start // step if right.shape[0] > blocks else 0
        right_spec = pl.BlockSpec((step, cols, channels), lambda b, h: (b + right_at, 0, 0))
    in_specs = [pl.BlockSpec((step, rows, channels), lambda b, h: (b + left_at, h[0], 0)), right_spec]
    args, aliases, out_at, out_blocks = [half, left, right], {}, 0, blocks
    if received is not None:
        in_specs.append(pl.BlockSpec((step, rows, cols), lambda b, h: (b, 0, 0)))
        args.append(received)
        out_at, out_blocks = start // step, total
        if into is not None:
            in_specs.append(pl.BlockSpec(memory_space=pl.ANY))
            aliases = {len(args): 0}
            args.append(into)
    return pl.pallas_call(
        outer_kernel,
        grid_spec=pltpu.PrefetchScalarGridSpec(
            num_scalar_prefetch=1,
            grid=(blocks // step,),
            in_specs=in_specs,
            out_specs=pl.BlockSpec((step, rows, cols), lambda b, h: (b + out_at, 0, 0)),
        ),
        out_shape=jax.ShapeDtypeStruct((out_blocks, rows, cols), jnp.bfloat16),
        input_output_aliases=aliases,
        compiler_params=pltpu.CompilerParams(vmem_limit_bytes=VMEM),
        cost_estimate=pl.CostEstimate(
            flops=2 * blocks * rows * cols * channels,
            bytes_accessed=2 * blocks * (rows * cols + rows * channels + cols * channels),
            transcendentals=0,
        ),
    )(*args)


def back_kernel(factor_ref, rows_ref, slope_ref, out_ref):
    product = lax.dot_general(
        factor_ref[0], rows_ref[0], (((0,), (0,)), ((), ())), preferred_element_type=jnp.float32
    )
    out_ref[...] = (product * slope_ref[...]).astype(jnp.bfloat16)


def back(factor, rows, slope, start):
    blocks, depth, channels = rows.shape
    width = factor.shape[2]
    return pl.pallas_call(
        back_kernel,
        grid=(blocks,),
        in_specs=[
            pl.BlockSpec((1, depth, width), lambda b: (b + start, 0, 0)),
            pl.BlockSpec((1, depth, channels), lambda b: (b, 0, 0)),
            pl.BlockSpec((width, channels), lambda b: (b + start, 0)),
        ],
        out_specs=pl.BlockSpec((width, channels), lambda b: (b, 0)),
        out_shape=jax.ShapeDtypeStruct((blocks * width, channels), jnp.bfloat16),
        compiler_params=pltpu.CompilerParams(vmem_limit_bytes=VMEM),
        cost_estimate=pl.CostEstimate(
            flops=WEIGHT * 2 * blocks * depth * width * channels,
            bytes_accessed=WEIGHT * 2 * blocks * (depth * width + depth * channels + 3 * width * channels),
            transcendentals=0,
        ),
    )(factor, rows, slope)


def signal_kernel(cuts_, taps, *refs):
    pieces, firsts = refs[: len(cuts_)], refs[len(cuts_) : 2 * len(cuts_)]
    following_ref, weight_ref, out_ref = refs[2 * len(cuts_) :]
    block, last = pl.program_id(0), pl.num_programs(0) - 1

    def spread(rows, next_rows):
        rows = rows[...].astype(jnp.float32)
        extended = jnp.concatenate([rows, next_rows[...].astype(jnp.float32)], axis=0)
        total = weight_ref[0:1, :] * rows
        for r in range(1, taps):
            ahead = pltpu.roll(extended, extended.shape[0] - r, 0)[: rows.shape[0]]
            total += weight_ref[r : r + 1, :] * ahead
        out_ref[...] = total.astype(jnp.bfloat16)

    for n, (start, size) in enumerate(cuts_):
        end = start + size - 1

        @pl.when((block >= start) & (block < end))
        def _():
            spread(pieces[n], firsts[n])

        @pl.when(block == end)
        def _():
            spread(pieces[n], following_ref if n == len(cuts_) - 1 else firsts[n + 1])


def signal_back(grad_conv, following, conv_weight, cuts_, rows):
    channels = conv_weight.shape[1]
    blocks = sum(size for _, size in cuts_)
    following = jnp.pad(following, ((0, ROW_TILE - following.shape[0]), (0, 0)))
    step = rows // ROW_TILE

    def own(start, size):
        return lambda b: (jnp.clip(b - start, 0, size - 1), 0)

    def first_rows(start, size):
        return lambda b: (jnp.clip(b + 1 - start, 0, size - 1) * step, 0)

    return pl.pallas_call(
        functools.partial(signal_kernel, cuts_, conv_weight.shape[0]),
        grid=(blocks,),
        in_specs=[pl.BlockSpec((rows, channels), own(*cut)) for cut in cuts_]
        + [pl.BlockSpec((ROW_TILE, channels), first_rows(*cut)) for cut in cuts_]
        + [
            pl.BlockSpec((ROW_TILE, channels), lambda b: (0, 0)),
            pl.BlockSpec(conv_weight.shape, lambda b: (0, 0)),
        ],
        out_specs=pl.BlockSpec((rows, channels), lambda b: (b, 0)),
        out_shape=jax.ShapeDtypeStruct((blocks * rows, channels), jnp.bfloat16),
        compiler_params=pltpu.CompilerParams(vmem_limit_bytes=VMEM),
        cost_estimate=pl.CostEstimate(
            flops=WEIGHT * 8 * blocks * rows * channels,
            bytes_accessed=WEIGHT * 4 * blocks * rows * channels,
            transcendentals=0,
        ),
    )(*grad_conv, *grad_conv, following, conv_weight)


def body(signal, conv_weight, first_factor, second_factor, grad_output):
    _, tok_rows, channels = signal.shape
    blocks, block_order = first_factor.shape[0], first_factor.shape[1]
    col_blocks, block_count = second_factor.shape[0], second_factor.shape[1]
    tap_count = conv_weight.shape[0]
    devices = lax.axis_size("seq")
    mine = lax.axis_index("batch")[None]
    theirs = 1 - mine
    tail = tap_count - 1

    first_cuts = cuts(blocks, (16, 16))
    second_cuts = cuts(col_blocks, (14, 10, 8))

    tied = lax.optimization_barrier

    def swapped(part):
        return lax.ppermute(part, "batch", [(0, 1), (1, 0)])

    def exchanged(sent):
        return lax.all_to_all(sent, "seq", 0, 0, tiled=True)

    def ordered(rows, size):
        return rows.reshape(block_order, size, channels).transpose(1, 0, 2)

    previous = passed_along(signal[0, tok_rows - tail :, :], "seq", 1)
    upstream = grad_output.reshape(col_blocks, block_count, channels)
    outgoing = split_product(second_factor, upstream, devices, first_cuts)
    *outgoing, previous = tied((*outgoing, previous))

    arrived = exchanged(outgoing[0])
    padded_in = jnp.concatenate([previous, signal[0]], axis=0).astype(jnp.float32)
    conv_out = sum(
        conv_weight[r][None, :] * padded_in[tail - r : tail - r + tok_rows, :] for r in range(tap_count)
    )
    gate_val = jax.nn.sigmoid(conv_out)
    hidden = (conv_out * gate_val).astype(jnp.bfloat16).reshape(blocks, block_order, channels)
    slope = gate_val * (1.0 + conv_out * (1.0 - gate_val))
    mixed = jnp.einsum(
        "ikj,ijd->ikd", first_factor, hidden, preferred_element_type=jnp.float32
    ).astype(jnp.bfloat16)
    by_owner = mixed.reshape(blocks, devices, col_blocks, channels).transpose(1, 2, 0, 3)
    pieces = [by_owner[:, start : start + size] for start, size in second_cuts]
    arrived, hidden, slope, *rest = tied((arrived, hidden, slope, *pieces, *outgoing[1:]))
    pieces, rest = rest[: len(pieces)], rest[len(pieces) :]

    row_blocks, got_first, grad_conv = [], [], []
    for (start, size), sent in zip(first_cuts, rest):
        coming = exchanged(sent)
        rows, part = tied((ordered(arrived, size), outer(theirs, ordered(arrived, size), hidden, start)))
        got = swapped(part)
        back_rows = back(first_factor, rows, slope, start)
        row_blocks.append(rows)
        arrived, hidden, back_rows, got, *pieces = tied((coming, hidden, back_rows, got, *pieces))
        got_first.append(got)
        grad_conv.append(back_rows)

    columns = exchanged(pieces[0])
    start, size = first_cuts[-1]
    rows, part = tied((ordered(arrived, size), outer(theirs, ordered(arrived, size), hidden, start)))
    got = swapped(part)
    back_rows = back(first_factor, rows, slope, start)
    following = passed_along((grad_conv + [back_rows])[0][:tail, :], "seq", -1)
    columns, following, got, back_rows, *pieces = tied((columns, following, got, back_rows, *pieces[1:]))
    row_blocks.append(rows)
    got_first.append(got)
    grad_conv.append(back_rows)

    arrived_columns, got_second = [], []
    for step, (start, size) in enumerate(second_cuts):
        coming = exchanged(pieces[step]) if pieces[step:] else None
        part = outer(theirs, upstream, columns, start)
        arrived_columns.append(columns)
        if step == 0:
            following, part = tied((following, part))
            grad_signal = signal_back(grad_conv, following, conv_weight, first_cuts, block_order)
        got = swapped(part)
        if coming is not None:
            columns, grad_signal, got, *rest = tied((coming, grad_signal, got, *pieces[step + 1 :]))
            pieces[step + 1 :] = rest
        got_second.append(got)

    grad_first = grad_second = None
    for (start, _), rows, got in zip(first_cuts, row_blocks, got_first):
        grad_first = outer(mine, rows, hidden, start, got, grad_first, blocks)
    for (start, _), columns, got in zip(second_cuts, arrived_columns, got_second):
        grad_second = outer(mine, upstream, columns, start, got, grad_second, col_blocks)
    return (
        grad_signal[None],
        grad_first,
        grad_second,
    )


def solution(mesh):
    placed = (
        P("batch", "seq", None),
        P(),
        P("seq", None, None),
        P("seq", None, None),
        P("batch", "seq", None),
    )
    return jax.shard_map(
        body,
        mesh=mesh,
        in_specs=placed,
        out_specs=(P("batch", "seq", None), P("seq", "batch", None), P("seq", "batch", None)),
        check_vma=False,
    )
```

```python
import functools

import jax
import jax.numpy as jnp
from jax import lax
from jax.experimental import pallas as pl
from jax.experimental.pallas import tpu as pltpu
from jax.sharding import PartitionSpec as P

ROW_TILE = 16
VMEM = 64 * 2**20 - 2**18
WEIGHT = 1


def passed_along(value, axis, steps):
    count = lax.axis_size(axis)
    initial, last = (max(0, -steps), min(count, count - steps))
    return lax.ppermute(value, axis, [(source, source + steps) for source in range(initial, last)])


def cuts(total, sizes):
    if sum(sizes) != total:
        sizes = (total,)
    return [(sum(sizes[:n]), size) for n, size in enumerate(sizes)]


def per_step(blocks, start=0):
    return next(n for n in (4, 2, 1) if blocks % n == 0 and start % n == 0)


def split_product_kernel(factor_ref, rows_ref, out_ref):
    devices = out_ref.shape[0]
    for n in range(factor_ref.shape[0]):
        product = lax.dot_general(
            factor_ref[n], rows_ref[n], (((0,), (0,)), ((), ())), preferred_element_type=jnp.float32
        ).astype(jnp.bfloat16)
        out_ref[:, n] = product.reshape(devices, product.shape[0] // devices, product.shape[1])


def split_product(factor, rows, devices, start, size):
    _, depth, width = factor.shape
    channels = rows.shape[2]
    part = width // devices
    if part % ROW_TILE:
        product = jnp.einsum(
            "kmi,kmd->kid",
            factor[start : start + size],
            rows[start : start + size],
            preferred_element_type=jnp.float32,
        ).astype(jnp.bfloat16)
        return product.reshape(size, devices, part, channels).transpose(1, 0, 2, 3)
    step = per_step(size, start)
    at = start // step
    return pl.pallas_call(
        split_product_kernel,
        grid=(size // step,),
        in_specs=[
            pl.BlockSpec((step, depth, width), lambda k: (k + at, 0, 0)),
            pl.BlockSpec((step, depth, channels), lambda k: (k + at, 0, 0)),
        ],
        out_specs=pl.BlockSpec((devices, step, part, channels), lambda k: (0, k, 0, 0)),
        out_shape=jax.ShapeDtypeStruct((devices, size, part, channels), jnp.bfloat16),
        compiler_params=pltpu.CompilerParams(vmem_limit_bytes=VMEM),
        cost_estimate=pl.CostEstimate(
            flops=2 * size * depth * width * channels,
            bytes_accessed=2 * size * (depth * width + depth * channels + width * channels),
            transcendentals=0,
        ),
    )(factor, rows)


def outer_kernel(half_ref, left_ref, right_ref, *refs):
    out_ref = refs[-1]
    channels = left_ref.shape[-1]
    for n in range(left_ref.shape[0]):
        right = right_ref[n] if len(right_ref.shape) == 3 else right_ref[:, n].reshape(-1, channels)
        product = lax.dot_general(
            left_ref[n], right, (((1,), (1,)), ((), ())), preferred_element_type=jnp.float32
        ).astype(jnp.bfloat16)
        if len(refs) == 1:
            out_ref[n] = product
        else:
            total = product.astype(jnp.float32) + refs[0][n].astype(jnp.float32)
            _, groups, _, rows, cols = out_ref.shape
            out_ref[n, :, 0] = total.astype(jnp.bfloat16).reshape(groups, rows, cols)


def outer(half, left, right, left_start=0, right_start=0, size=None, target=None):
    halves = lax.axis_size("batch")
    rows, channels = left.shape[1] // halves, left.shape[2]
    if right.ndim == 4 and right.shape[2] % ROW_TILE:
        right = right.transpose(1, 0, 2, 3).reshape(right.shape[1], -1, channels)
    out_start = target[3] if target else 0
    step = next(n for n in (4, 2, 1) if not any(v % n for v in (size, left_start, right_start, out_start)))
    left_at, right_at, out_at = left_start // step, right_start // step, out_start // step
    if right.ndim == 4:
        devices, _, part, _ = right.shape
        cols = devices * part
        right_spec = pl.BlockSpec((devices, step, part, channels), lambda b, h: (0, b + right_at, 0, 0))
    else:
        cols = right.shape[1]
        right_spec = pl.BlockSpec((step, cols, channels), lambda b, h: (b + right_at, 0, 0))
    in_specs = [pl.BlockSpec((step, rows, channels), lambda b, h: (b + left_at, h[0], 0)), right_spec]
    args, aliases = [half, left, right], {}
    if target is None:
        shape, out_spec = (size, rows, cols), pl.BlockSpec((step, rows, cols), lambda b, h: (b, 0, 0))
    else:
        received, into, (blocks, groups, pieces), _, piece = target
        shape = (blocks, groups, pieces, rows // groups, cols)
        out_spec = pl.BlockSpec(
            (step, groups, 1, rows // groups, cols), lambda b, h: (b + out_at, 0, piece, 0, 0)
        )
        in_specs.append(pl.BlockSpec((step, rows, cols), lambda b, h: (b, 0, 0)))
        args.append(received)
        if into is not None:
            in_specs.append(pl.BlockSpec(memory_space=pl.ANY))
            aliases = {len(args): 0}
            args.append(into)
    return pl.pallas_call(
        outer_kernel,
        grid_spec=pltpu.PrefetchScalarGridSpec(
            num_scalar_prefetch=1, grid=(size // step,), in_specs=in_specs, out_specs=out_spec
        ),
        out_shape=jax.ShapeDtypeStruct(shape, jnp.bfloat16),
        input_output_aliases=aliases,
        compiler_params=pltpu.CompilerParams(vmem_limit_bytes=VMEM),
        cost_estimate=pl.CostEstimate(
            flops=2 * size * rows * cols * channels,
            bytes_accessed=2 * size * (rows * cols + rows * channels + cols * channels),
            transcendentals=0,
        ),
    )(*args)


def back_kernel(groups, factor_ref, slope_ref, *refs):
    *rows_refs, out_ref = refs
    blocks, depth, width = factor_ref.shape
    share = depth // groups // len(rows_refs)
    for n in range(blocks):
        factor = factor_ref[n].reshape(groups, len(rows_refs), share, width)
        total = sum(
            lax.dot_general(
                factor[:, piece].reshape(groups * share, width),
                rows_ref[n],
                (((0,), (0,)), ((), ())),
                preferred_element_type=jnp.float32,
            )
            for piece, rows_ref in enumerate(rows_refs)
        )
        at = pl.ds(n * width, width)
        out_ref[at] = (total * slope_ref[at]).astype(jnp.bfloat16)


def back(factor, pieces, slope, groups):
    blocks, depth, width = factor.shape
    channels = slope.shape[1]
    step = 2 if blocks % 2 == 0 else 1
    return pl.pallas_call(
        functools.partial(back_kernel, groups),
        grid=(blocks // step,),
        in_specs=[
            pl.BlockSpec((step, depth, width), lambda b: (b, 0, 0)),
            pl.BlockSpec((step * width, channels), lambda b: (b, 0)),
        ]
        + [pl.BlockSpec((step, *rows.shape[1:]), lambda b: (b, 0, 0)) for rows in pieces],
        out_specs=pl.BlockSpec((step * width, channels), lambda b: (b, 0)),
        out_shape=jax.ShapeDtypeStruct((blocks * width, channels), jnp.bfloat16),
        compiler_params=pltpu.CompilerParams(vmem_limit_bytes=VMEM),
        cost_estimate=pl.CostEstimate(
            flops=2 * blocks * depth * width * channels,
            bytes_accessed=2 * blocks * (depth * width + depth * channels + 3 * width * channels),
            transcendentals=0,
        ),
    )(factor, slope, *pieces)


def signal_kernel(cuts_, taps, *refs):
    pieces, firsts = refs[: len(cuts_)], refs[len(cuts_) : 2 * len(cuts_)]
    following_ref, weight_ref, out_ref = refs[2 * len(cuts_) :]
    block, last = pl.program_id(0), pl.num_programs(0) - 1

    def spread(rows, next_rows):
        rows = rows[...].astype(jnp.float32)
        extended = jnp.concatenate([rows, next_rows[...].astype(jnp.float32)], axis=0)
        total = weight_ref[0:1, :] * rows
        for r in range(1, taps):
            ahead = pltpu.roll(extended, extended.shape[0] - r, 0)[: rows.shape[0]]
            total += weight_ref[r : r + 1, :] * ahead
        out_ref[...] = total.astype(jnp.bfloat16)

    for n, (start, size) in enumerate(cuts_):
        end = start + size - 1

        @pl.when((block >= start) & (block < end))
        def _():
            spread(pieces[n], firsts[n])

        @pl.when(block == end)
        def _():
            spread(pieces[n], following_ref if n == len(cuts_) - 1 else firsts[n + 1])


def signal_back(grad_conv, following, conv_weight, cuts_, rows):
    channels = conv_weight.shape[1]
    blocks = sum(size for _, size in cuts_)
    following = jnp.pad(following, ((0, ROW_TILE - following.shape[0]), (0, 0)))
    step = rows // ROW_TILE

    def own(start, size):
        return lambda b: (jnp.clip(b - start, 0, size - 1), 0)

    def first_rows(start, size):
        return lambda b: (jnp.clip(b + 1 - start, 0, size - 1) * step, 0)

    return pl.pallas_call(
        functools.partial(signal_kernel, cuts_, conv_weight.shape[0]),
        grid=(blocks,),
        in_specs=[pl.BlockSpec((rows, channels), own(*cut)) for cut in cuts_]
        + [pl.BlockSpec((ROW_TILE, channels), first_rows(*cut)) for cut in cuts_]
        + [
            pl.BlockSpec((ROW_TILE, channels), lambda b: (0, 0)),
            pl.BlockSpec(conv_weight.shape, lambda b: (0, 0)),
        ],
        out_specs=pl.BlockSpec((rows, channels), lambda b: (b, 0)),
        out_shape=jax.ShapeDtypeStruct((blocks * rows, channels), jnp.bfloat16),
        compiler_params=pltpu.CompilerParams(vmem_limit_bytes=VMEM),
        cost_estimate=pl.CostEstimate(
            flops=WEIGHT * 8 * blocks * rows * channels,
            bytes_accessed=WEIGHT * 4 * blocks * rows * channels,
            transcendentals=0,
        ),
    )(*grad_conv, *grad_conv, following, conv_weight)


def body(signal, conv_weight, first_factor, second_factor, grad_output):
    _, tok_rows, channels = signal.shape
    blocks, block_order = first_factor.shape[0], first_factor.shape[1]
    col_blocks, block_count = second_factor.shape[0], second_factor.shape[1]
    tap_count = conv_weight.shape[0]
    devices = lax.axis_size("seq")
    mine = lax.axis_index("batch")[None]
    theirs = 1 - mine
    tail = tap_count - 1

    first_cuts = cuts(col_blocks, (16, 16))
    second_cuts = cuts(col_blocks, (13, 9, 6, 4))
    tied = lax.optimization_barrier

    def swapped(part):
        return lax.ppermute(part, "batch", [(0, 1), (1, 0)])

    def exchanged(sent):
        return lax.all_to_all(sent, "seq", 0, 0, tiled=True)

    def ordered(rows):
        return rows.reshape(-1, blocks, channels).transpose(1, 0, 2)

    previous = passed_along(signal[0, tok_rows - tail :, :], "seq", 1)
    upstream = grad_output.reshape(col_blocks, block_count, channels)
    sent = split_product(second_factor, upstream, devices, *first_cuts[0])
    sent, previous = tied((sent, previous))

    arrived = exchanged(sent)
    padded_in = jnp.concatenate([previous, signal[0]], axis=0).astype(jnp.float32)
    conv_out = sum(
        conv_weight[r][None, :] * padded_in[tail - r : tail - r + tok_rows, :] for r in range(tap_count)
    )
    later, conv_out = tied((upstream, conv_out))
    rest = [split_product(second_factor, later, devices, *cut) for cut in first_cuts[1:]]
    gate_val = jax.nn.sigmoid(conv_out)
    hidden = (conv_out * gate_val).astype(jnp.bfloat16).reshape(blocks, block_order, channels)
    slope = gate_val * (1.0 + conv_out * (1.0 - gate_val))
    mixed = jnp.einsum(
        "ikj,ijd->ikd", first_factor, hidden, preferred_element_type=jnp.float32
    ).astype(jnp.bfloat16)
    by_owner = mixed.reshape(blocks, devices, col_blocks, channels).transpose(1, 2, 0, 3)
    pieces = [by_owner[:, start : start + size] for start, size in second_cuts]
    arrived, hidden, slope, *rest = tied((arrived, hidden, slope, *pieces, *rest))
    pieces, rest = rest[: len(pieces)], rest[len(pieces) :]

    shape_first = (blocks, devices // lax.axis_size("batch"), len(first_cuts))
    row_pieces, got_first, grad_first = [], [], None
    for sent in rest:
        coming = exchanged(sent)
        rows = ordered(arrived)
        got = swapped(outer(theirs, rows, hidden, size=blocks))
        arrived, rows, got, hidden, *pieces = tied((coming, rows, got, hidden, *pieces))
        row_pieces.append(rows)
        got_first.append(got)

    columns = exchanged(pieces[0])
    rows = ordered(arrived)
    rows, part = tied((rows, outer(theirs, rows, hidden, size=blocks)))
    got = swapped(part)
    row_pieces.append(rows)
    grad_conv = back(first_factor, row_pieces, slope, devices)
    following = passed_along(grad_conv[:tail, :], "seq", -1)
    for piece, earlier in enumerate(got_first):
        grad_first = outer(
            mine, row_pieces[piece], hidden, size=blocks, target=(earlier, grad_first, shape_first, 0, piece)
        )
    state = (columns, following, got, grad_conv, *pieces[1:])
    if got_first:
        state += (grad_first,)
    state = tied(state)
    columns, following, got, grad_conv, *pieces = state[: 4 + len(pieces) - 1]
    if got_first:
        grad_first = state[-1]

    shape_second = (col_blocks, 1, 1)
    grad_second = grad_signal = None
    held = []
    last_first = (got, grad_first, shape_first, 0, len(first_cuts) - 1)
    summing = []

    def own_half(start, at, size, columns, got):
        return lambda into: outer(
            mine, upstream, columns, start, at, size, target=(got, into, shape_second, start, 0)
        )

    for step, (start, size) in enumerate(second_cuts):
        coming = exchanged(pieces[step]) if pieces[step:] else None
        back_size = 1 if coming is not None else 0
        early = size - back_size
        part = outer(theirs, upstream, columns, start, 0, early)
        late_part = outer(theirs, upstream, columns, start + early, early, back_size) if back_size else None
        got_late = [(s0, a0, n0, c0, swapped(p0)) for s0, a0, n0, c0, p0 in held]
        if got_late:
            part, sent_late = tied((part, got_late[0][4]))
            got_late = [(*got_late[0][:4], sent_late)]
        got = swapped(part)
        if step == 0:
            grad_first = outer(mine, row_pieces[-1], hidden, size=blocks, target=last_first)
            grad_signal = signal_back([grad_conv], following, conv_weight, [(0, blocks)], block_order)
        if coming is not None:
            for add in summing:
                grad_second = add(grad_second)
            summing = []
        if coming is not None:
            state = [coming, got, late_part, grad_signal, grad_first, *pieces[step + 1 :]]
            state += [entry[4] for entry in got_late]
            if grad_second is not None:
                state.append(grad_second)
            state = list(tied(tuple(state)))
            if grad_second is not None:
                grad_second = state.pop()
            got_late = [(*entry[:4], state.pop()) for entry in got_late[::-1]]
            following_columns, got, late_part, grad_signal, grad_first, *rest = state
            pieces[step + 1 :] = rest
            held = [(start + early, early, back_size, columns, late_part)]
        summing += [own_half(*entry) for entry in got_late] + [own_half(start, 0, early, columns, got)]
        if coming is not None:
            columns = following_columns
    for add in summing:
        grad_second = add(grad_second)
    grad_first = grad_first.reshape(blocks, -1, block_order)
    grad_second = grad_second.reshape(col_blocks, -1, block_count)
    return (
        grad_signal[None],
        grad_first,
        grad_second,
    )


def solution(mesh):
    placed = (
        P("batch", "seq", None),
        P(),
        P("seq", None, None),
        P("seq", None, None),
        P("batch", "seq", None),
    )
    return jax.shard_map(
        body,
        mesh=mesh,
        in_specs=placed,
        out_specs=(P("batch", "seq", None), P("seq", "batch", None), P("seq", "batch", None)),
        check_vma=False,
    )
```

```python
import functools

import jax
import jax.numpy as jnp
from jax import lax
from jax.experimental import pallas as pl
from jax.experimental.pallas import tpu as pltpu
from jax.sharding import PartitionSpec as P

ROW_TILE = 16
VMEM = 64 * 2**20 - 2**18
WEIGHT = 1


def passed_along(value, axis, steps):
    count = lax.axis_size(axis)
    initial, last = (max(0, -steps), min(count, count - steps))
    return lax.ppermute(value, axis, [(source, source + steps) for source in range(initial, last)])


def cuts(total, sizes):
    if sum(sizes) != total:
        sizes = (total,)
    return [(sum(sizes[:n]), size) for n, size in enumerate(sizes)]


def per_step(blocks, start=0):
    return next(n for n in (4, 2, 1) if blocks % n == 0 and start % n == 0)


def split_product_kernel(factor_ref, rows_ref, out_ref):
    devices = out_ref.shape[0]
    for n in range(factor_ref.shape[0]):
        product = lax.dot_general(
            factor_ref[n], rows_ref[n], (((0,), (0,)), ((), ())), preferred_element_type=jnp.float32
        ).astype(jnp.bfloat16)
        out_ref[:, n] = product.reshape(devices, product.shape[0] // devices, product.shape[1])


def split_product(factor, rows, devices, start, size):
    _, depth, width = factor.shape
    channels = rows.shape[2]
    part = width // devices
    if part % ROW_TILE:
        product = jnp.einsum(
            "kmi,kmd->kid",
            factor[start : start + size],
            rows[start : start + size],
            preferred_element_type=jnp.float32,
        ).astype(jnp.bfloat16)
        return product.reshape(size, devices, part, channels).transpose(1, 0, 2, 3)
    step = per_step(size, start)
    at = start // step
    return pl.pallas_call(
        split_product_kernel,
        grid=(size // step,),
        in_specs=[
            pl.BlockSpec((step, depth, width), lambda k: (k + at, 0, 0)),
            pl.BlockSpec((step, depth, channels), lambda k: (k + at, 0, 0)),
        ],
        out_specs=pl.BlockSpec((devices, step, part, channels), lambda k: (0, k, 0, 0)),
        out_shape=jax.ShapeDtypeStruct((devices, size, part, channels), jnp.bfloat16),
        compiler_params=pltpu.CompilerParams(vmem_limit_bytes=VMEM),
        cost_estimate=pl.CostEstimate(
            flops=2 * size * depth * width * channels,
            bytes_accessed=2 * size * (depth * width + depth * channels + width * channels),
            transcendentals=0,
        ),
    )(factor, rows)


def outer_kernel(half_ref, left_ref, right_ref, *refs):
    out_ref = refs[-1]
    channels = left_ref.shape[-1]
    for n in range(left_ref.shape[0]):
        right = right_ref[n] if len(right_ref.shape) == 3 else right_ref[:, n].reshape(-1, channels)
        product = lax.dot_general(
            left_ref[n], right, (((1,), (1,)), ((), ())), preferred_element_type=jnp.float32
        ).astype(jnp.bfloat16)
        if len(refs) == 1:
            out_ref[n] = product
        else:
            total = product.astype(jnp.float32) + refs[0][n].astype(jnp.float32)
            _, groups, _, rows, cols = out_ref.shape
            out_ref[n, :, 0] = total.astype(jnp.bfloat16).reshape(groups, rows, cols)


def outer(half, left, right, left_start=0, right_start=0, size=None, target=None):
    halves = lax.axis_size("batch")
    rows, channels = left.shape[1] // halves, left.shape[2]
    if right.ndim == 4 and right.shape[2] % ROW_TILE:
        right = right.transpose(1, 0, 2, 3).reshape(right.shape[1], -1, channels)
    out_start = target[3] if target else 0
    step = next(n for n in (4, 5, 2, 1) if not any(v % n for v in (size, right_start, out_start)))
    right_at, out_at = right_start // step, out_start // step
    if right.ndim == 4:
        devices, _, part, _ = right.shape
        cols = devices * part
        right_spec = pl.BlockSpec((devices, step, part, channels), lambda b, h: (0, b + right_at, 0, 0))
    else:
        cols = right.shape[1]
        right_spec = pl.BlockSpec((step, cols, channels), lambda b, h: (b + right_at, 0, 0))
    left_block = tuple(pl.Element(n) for n in (step, rows, channels))
    left_spec = pl.BlockSpec(left_block, lambda b, h: (b * step + left_start, pl.multiple_of(h[0] * rows, rows), 0))
    in_specs = [left_spec, right_spec]
    args, aliases = [half, left, right], {}
    if target is None:
        shape, out_spec = (size, rows, cols), pl.BlockSpec((step, rows, cols), lambda b, h: (b, 0, 0))
    else:
        received, into, (blocks, groups, pieces), _, piece = target
        shape = (blocks, groups, pieces, rows // groups, cols)
        out_spec = pl.BlockSpec(
            (step, groups, 1, rows // groups, cols), lambda b, h: (b + out_at, 0, piece, 0, 0)
        )
        in_specs.append(pl.BlockSpec((step, rows, cols), lambda b, h: (b, 0, 0)))
        args.append(received)
        if into is not None:
            in_specs.append(pl.BlockSpec(memory_space=pl.ANY))
            aliases = {len(args): 0}
            args.append(into)
    return pl.pallas_call(
        outer_kernel,
        grid_spec=pltpu.PrefetchScalarGridSpec(
            num_scalar_prefetch=1, grid=(size // step,), in_specs=in_specs, out_specs=out_spec
        ),
        out_shape=jax.ShapeDtypeStruct(shape, jnp.bfloat16),
        input_output_aliases=aliases,
        compiler_params=pltpu.CompilerParams(vmem_limit_bytes=VMEM),
        cost_estimate=pl.CostEstimate(
            flops=2 * size * rows * cols * channels,
            bytes_accessed=2 * size * (rows * cols + rows * channels + cols * channels),
            transcendentals=0,
        ),
    )(*args)


def back_kernel(groups, factor_ref, slope_ref, *refs):
    *rows_refs, out_ref = refs
    blocks, depth, width = factor_ref.shape
    share = depth // groups // len(rows_refs)
    for n in range(blocks):
        factor = factor_ref[n].reshape(groups, len(rows_refs), share, width)
        total = sum(
            lax.dot_general(
                factor[:, piece].reshape(groups * share, width),
                rows_ref[n],
                (((0,), (0,)), ((), ())),
                preferred_element_type=jnp.float32,
            )
            for piece, rows_ref in enumerate(rows_refs)
        )
        at = pl.ds(n * width, width)
        out_ref[at] = (total * slope_ref[at]).astype(jnp.bfloat16)


def back(factor, pieces, slope, groups):
    blocks, depth, width = factor.shape
    channels = slope.shape[1]
    step = 2 if blocks % 2 == 0 else 1
    return pl.pallas_call(
        functools.partial(back_kernel, groups),
        grid=(blocks // step,),
        in_specs=[
            pl.BlockSpec((step, depth, width), lambda b: (b, 0, 0)),
            pl.BlockSpec((step * width, channels), lambda b: (b, 0)),
        ]
        + [pl.BlockSpec((step, *rows.shape[1:]), lambda b: (b, 0, 0)) for rows in pieces],
        out_specs=pl.BlockSpec((step * width, channels), lambda b: (b, 0)),
        out_shape=jax.ShapeDtypeStruct((blocks * width, channels), jnp.bfloat16),
        compiler_params=pltpu.CompilerParams(vmem_limit_bytes=VMEM),
        cost_estimate=pl.CostEstimate(
            flops=2 * blocks * depth * width * channels,
            bytes_accessed=2 * blocks * (depth * width + depth * channels + 3 * width * channels),
            transcendentals=0,
        ),
    )(factor, slope, *pieces)


def gate_kernel(taps, rows_ref, before_ref, previous_ref, weight_ref, hidden_ref, slope_ref):
    rows = rows_ref[...].astype(jnp.float32)

    def write(before):
        extended = jnp.concatenate([before[...].astype(jnp.float32), rows], axis=0)
        conv = weight_ref[0:1, :] * rows
        for r in range(1, taps):
            conv += weight_ref[r : r + 1, :] * pltpu.roll(extended, r, 0)[before.shape[0] :]
        gate = jax.nn.sigmoid(conv)
        hidden_ref[...] = (conv * gate).astype(jnp.bfloat16)
        slope_ref[...] = gate * (1.0 + conv * (1.0 - gate))

    @pl.when(pl.program_id(0) == 0)
    def _():
        write(previous_ref)

    @pl.when(pl.program_id(0) > 0)
    def _():
        write(before_ref)


def gated(signal, previous, conv_weight, rows):
    tokens, channels = signal.shape
    previous = jnp.pad(previous, ((ROW_TILE - previous.shape[0], 0), (0, 0)))
    step = rows // ROW_TILE
    whole = pl.BlockSpec((rows, channels), lambda b: (b, 0))
    return pl.pallas_call(
        functools.partial(gate_kernel, conv_weight.shape[0]),
        grid=(tokens // rows,),
        in_specs=[
            whole,
            pl.BlockSpec((ROW_TILE, channels), lambda b: (jnp.maximum(b * step - 1, 0), 0)),
            pl.BlockSpec((ROW_TILE, channels), lambda b: (0, 0)),
            pl.BlockSpec(conv_weight.shape, lambda b: (0, 0)),
        ],
        out_specs=[whole, whole],
        out_shape=[
            jax.ShapeDtypeStruct((tokens, channels), jnp.bfloat16),
            jax.ShapeDtypeStruct((tokens, channels), jnp.float32),
        ],
        compiler_params=pltpu.CompilerParams(vmem_limit_bytes=VMEM),
        cost_estimate=pl.CostEstimate(
            flops=20 * tokens * channels, bytes_accessed=8 * tokens * channels, transcendentals=tokens * channels
        ),
    )(signal, signal, previous, conv_weight)


def signal_kernel(cuts_, taps, *refs):
    pieces, firsts = refs[: len(cuts_)], refs[len(cuts_) : 2 * len(cuts_)]
    following_ref, weight_ref, out_ref = refs[2 * len(cuts_) :]
    block, last = pl.program_id(0), pl.num_programs(0) - 1

    def spread(rows, next_rows):
        rows = rows[...].astype(jnp.float32)
        extended = jnp.concatenate([rows, next_rows[...].astype(jnp.float32)], axis=0)
        total = weight_ref[0:1, :] * rows
        for r in range(1, taps):
            ahead = pltpu.roll(extended, extended.shape[0] - r, 0)[: rows.shape[0]]
            total += weight_ref[r : r + 1, :] * ahead
        out_ref[...] = total.astype(jnp.bfloat16)

    for n, (start, size) in enumerate(cuts_):
        end = start + size - 1

        @pl.when((block >= start) & (block < end))
        def _():
            spread(pieces[n], firsts[n])

        @pl.when(block == end)
        def _():
            spread(pieces[n], following_ref if n == len(cuts_) - 1 else firsts[n + 1])


def signal_back(grad_conv, following, conv_weight, cuts_, rows):
    channels = conv_weight.shape[1]
    blocks = sum(size for _, size in cuts_)
    following = jnp.pad(following, ((0, ROW_TILE - following.shape[0]), (0, 0)))
    step = rows // ROW_TILE

    def own(start, size):
        return lambda b: (jnp.clip(b - start, 0, size - 1), 0)

    def first_rows(start, size):
        return lambda b: (jnp.clip(b + 1 - start, 0, size - 1) * step, 0)

    return pl.pallas_call(
        functools.partial(signal_kernel, cuts_, conv_weight.shape[0]),
        grid=(blocks,),
        in_specs=[pl.BlockSpec((rows, channels), own(*cut)) for cut in cuts_]
        + [pl.BlockSpec((ROW_TILE, channels), first_rows(*cut)) for cut in cuts_]
        + [
            pl.BlockSpec((ROW_TILE, channels), lambda b: (0, 0)),
            pl.BlockSpec(conv_weight.shape, lambda b: (0, 0)),
        ],
        out_specs=pl.BlockSpec((rows, channels), lambda b: (b, 0)),
        out_shape=jax.ShapeDtypeStruct((blocks * rows, channels), jnp.bfloat16),
        compiler_params=pltpu.CompilerParams(vmem_limit_bytes=VMEM),
        cost_estimate=pl.CostEstimate(
            flops=WEIGHT * 8 * blocks * rows * channels,
            bytes_accessed=WEIGHT * 4 * blocks * rows * channels,
            transcendentals=0,
        ),
    )(*grad_conv, *grad_conv, following, conv_weight)


def body(signal, conv_weight, first_factor, second_factor, grad_output):
    _, tok_rows, channels = signal.shape
    blocks, block_order = first_factor.shape[0], first_factor.shape[1]
    col_blocks, block_count = second_factor.shape[0], second_factor.shape[1]
    tap_count = conv_weight.shape[0]
    devices = lax.axis_size("seq")
    mine = lax.axis_index("batch")[None]
    theirs = 1 - mine
    tail = tap_count - 1

    first_cuts = cuts(col_blocks, (16, 16))
    second_cuts = cuts(col_blocks, (13, 9, 6, 4))
    tied = lax.optimization_barrier

    def swapped(part):
        return lax.ppermute(part, "batch", [(0, 1), (1, 0)])

    def exchanged(sent):
        return lax.all_to_all(sent, "seq", 0, 0, tiled=True)

    def ordered(rows):
        return rows.reshape(-1, blocks, channels).transpose(1, 0, 2)

    previous = passed_along(signal[0, tok_rows - tail :, :], "seq", 1)
    upstream = grad_output.reshape(col_blocks, block_count, channels)
    sent = split_product(second_factor, upstream, devices, *first_cuts[0])
    sent, previous = tied((sent, previous))

    arrived = exchanged(sent)
    hidden, slope = gated(signal[0], previous, conv_weight, block_order)
    later, hidden = tied((upstream, hidden))
    rest = [split_product(second_factor, later, devices, *cut) for cut in first_cuts[1:]]
    hidden = hidden.reshape(blocks, block_order, channels)
    mixed = jnp.einsum(
        "ikj,ijd->ikd", first_factor, hidden, preferred_element_type=jnp.float32
    ).astype(jnp.bfloat16)
    by_owner = mixed.reshape(blocks, devices, col_blocks, channels).transpose(1, 2, 0, 3)
    pieces = [by_owner[:, start : start + size] for start, size in second_cuts]
    arrived, hidden, slope, *rest = tied((arrived, hidden, slope, *pieces, *rest))
    pieces, rest = rest[: len(pieces)], rest[len(pieces) :]

    shape_first = (blocks, devices // lax.axis_size("batch"), len(first_cuts))
    row_pieces, got_first, grad_first = [], [], None
    for sent in rest:
        coming = exchanged(sent)
        rows = ordered(arrived)
        got = swapped(outer(theirs, rows, hidden, size=blocks))
        arrived, rows, got, hidden, *pieces = tied((coming, rows, got, hidden, *pieces))
        row_pieces.append(rows)
        got_first.append(got)

    columns = exchanged(pieces[0])
    rows = ordered(arrived)
    rows, part = tied((rows, outer(theirs, rows, hidden, size=blocks)))
    got = swapped(part)
    row_pieces.append(rows)
    grad_conv = back(first_factor, row_pieces, slope, devices)
    following = passed_along(grad_conv[:tail, :], "seq", -1)
    for piece, earlier in enumerate(got_first):
        grad_first = outer(
            mine, row_pieces[piece], hidden, size=blocks, target=(earlier, grad_first, shape_first, 0, piece)
        )
    state = (columns, following, got, grad_conv, *pieces[1:])
    if got_first:
        state += (grad_first,)
    state = tied(state)
    columns, following, got, grad_conv, *pieces = state[: 4 + len(pieces) - 1]
    if got_first:
        grad_first = state[-1]

    shape_second = (col_blocks, 1, 1)
    grad_second = grad_signal = None
    held = []
    last_first = (got, grad_first, shape_first, 0, len(first_cuts) - 1)
    summing = []

    def own_half(start, at, size, columns, got):
        return lambda into: outer(
            mine, upstream, columns, start, at, size, target=(got, into, shape_second, start, 0)
        )

    for step, (start, size) in enumerate(second_cuts):
        coming = exchanged(pieces[step]) if pieces[step:] else None
        back_size = 1 if coming is not None else 0
        early = size - back_size
        part = outer(theirs, upstream, columns, start, 0, early)
        late_part = outer(theirs, upstream, columns, start + early, early, back_size) if back_size else None
        got_late = [(s0, a0, n0, c0, swapped(p0)) for s0, a0, n0, c0, p0 in held]
        if got_late:
            part, sent_late = tied((part, got_late[0][4]))
            got_late = [(*got_late[0][:4], sent_late)]
        got = swapped(part)
        if step == 0:
            grad_first = outer(mine, row_pieces[-1], hidden, size=blocks, target=last_first)
            grad_signal = signal_back([grad_conv], following, conv_weight, [(0, blocks)], block_order)
        if coming is not None:
            for add in summing:
                grad_second = add(grad_second)
            summing = []
        if coming is not None:
            state = [coming, got, late_part, grad_signal, grad_first, *pieces[step + 1 :]]
            state += [entry[4] for entry in got_late]
            if grad_second is not None:
                state.append(grad_second)
            state = list(tied(tuple(state)))
            if grad_second is not None:
                grad_second = state.pop()
            got_late = [(*entry[:4], state.pop()) for entry in got_late[::-1]]
            following_columns, got, late_part, grad_signal, grad_first, *rest = state
            pieces[step + 1 :] = rest
            held = [(start + early, early, back_size, columns, late_part)]
        summing += [own_half(*entry) for entry in got_late] + [own_half(start, 0, early, columns, got)]
        if coming is not None:
            columns = following_columns
    for add in summing:
        grad_second = add(grad_second)
    grad_first = grad_first.reshape(blocks, -1, block_order)
    grad_second = grad_second.reshape(col_blocks, -1, block_count)
    return (
        grad_signal[None],
        grad_first,
        grad_second,
    )


def solution(mesh):
    placed = (
        P("batch", "seq", None),
        P(),
        P("seq", None, None),
        P("seq", None, None),
        P("batch", "seq", None),
    )
    return jax.shard_map(
        body,
        mesh=mesh,
        in_specs=placed,
        out_specs=(P("batch", "seq", None), P("seq", "batch", None), P("seq", "batch", None)),
        check_vma=False,
    )
```

```python
import functools

import jax
import jax.numpy as jnp
from jax import lax
from jax.experimental import pallas as pl
from jax.experimental.pallas import tpu as pltpu
from jax.sharding import PartitionSpec as P

ROW_TILE = 16
VMEM = 64 * 2**20 - 2**18
WEIGHT = 1


def passed_along(value, axis, steps):
    count = lax.axis_size(axis)
    initial, last = (max(0, -steps), min(count, count - steps))
    return lax.ppermute(value, axis, [(source, source + steps) for source in range(initial, last)])


def cuts(total, sizes):
    if sum(sizes) != total:
        sizes = (total,)
    return [(sum(sizes[:n]), size) for n, size in enumerate(sizes)]


def per_step(blocks, start=0):
    return next(n for n in (4, 2, 1) if blocks % n == 0 and start % n == 0)


def split_product_kernel(factor_ref, rows_ref, out_ref):
    devices = out_ref.shape[0]
    for n in range(factor_ref.shape[0]):
        product = lax.dot_general(
            factor_ref[n], rows_ref[n], (((0,), (0,)), ((), ())), preferred_element_type=jnp.float32
        ).astype(jnp.bfloat16)
        out_ref[:, n] = product.reshape(devices, product.shape[0] // devices, product.shape[1])


def split_product(factor, rows, devices, start, size):
    _, depth, width = factor.shape
    channels = rows.shape[2]
    part = width // devices
    if part % ROW_TILE:
        product = jnp.einsum(
            "kmi,kmd->kid",
            factor[start : start + size],
            rows[start : start + size],
            preferred_element_type=jnp.float32,
        ).astype(jnp.bfloat16)
        return product.reshape(size, devices, part, channels).transpose(1, 0, 2, 3)
    step = per_step(size, start)
    at = start // step
    return pl.pallas_call(
        split_product_kernel,
        grid=(size // step,),
        in_specs=[
            pl.BlockSpec((step, depth, width), lambda k: (k + at, 0, 0)),
            pl.BlockSpec((step, depth, channels), lambda k: (k + at, 0, 0)),
        ],
        out_specs=pl.BlockSpec((devices, step, part, channels), lambda k: (0, k, 0, 0)),
        out_shape=jax.ShapeDtypeStruct((devices, size, part, channels), jnp.bfloat16),
        compiler_params=pltpu.CompilerParams(vmem_limit_bytes=VMEM),
        cost_estimate=pl.CostEstimate(
            flops=2 * size * depth * width * channels,
            bytes_accessed=2 * size * (depth * width + depth * channels + width * channels),
            transcendentals=0,
        ),
    )(factor, rows)


def outer_kernel(half_ref, left_ref, right_ref, *refs):
    out_ref = refs[-1]
    channels = left_ref.shape[-1]
    for n in range(left_ref.shape[0]):
        right = right_ref[n] if len(right_ref.shape) == 3 else right_ref[:, n].reshape(-1, channels)
        product = lax.dot_general(
            left_ref[n], right, (((1,), (1,)), ((), ())), preferred_element_type=jnp.float32
        ).astype(jnp.bfloat16)
        if len(refs) == 1:
            out_ref[n] = product
        else:
            total = product.astype(jnp.float32) + refs[0][n].astype(jnp.float32)
            _, groups, _, rows, cols = out_ref.shape
            out_ref[n, :, 0] = total.astype(jnp.bfloat16).reshape(groups, rows, cols)


def outer(half, left, right, left_start=0, right_start=0, size=None, target=None):
    halves = lax.axis_size("batch")
    rows, channels = left.shape[1] // halves, left.shape[2]
    if right.ndim == 4 and right.shape[2] % ROW_TILE:
        right = right.transpose(1, 0, 2, 3).reshape(right.shape[1], -1, channels)
    out_start = target[3] if target else 0
    step = next(n for n in (4, 5, 2, 1) if not any(v % n for v in (size, right_start, out_start)))
    right_at, out_at = right_start // step, out_start // step
    if right.ndim == 4:
        devices, _, part, _ = right.shape
        cols = devices * part
        right_spec = pl.BlockSpec((devices, step, part, channels), lambda b, h: (0, b + right_at, 0, 0))
    else:
        cols = right.shape[1]
        right_spec = pl.BlockSpec((step, cols, channels), lambda b, h: (b + right_at, 0, 0))
    left_block = tuple(pl.Element(n) for n in (step, rows, channels))
    left_spec = pl.BlockSpec(left_block, lambda b, h: (b * step + left_start, pl.multiple_of(h[0] * rows, rows), 0))
    in_specs = [left_spec, right_spec]
    args, aliases = [half, left, right], {}
    if target is None:
        shape, out_spec = (size, rows, cols), pl.BlockSpec((step, rows, cols), lambda b, h: (b, 0, 0))
    else:
        received, into, (blocks, groups, pieces), _, piece = target
        shape = (blocks, groups, pieces, rows // groups, cols)
        out_spec = pl.BlockSpec(
            (step, groups, 1, rows // groups, cols), lambda b, h: (b + out_at, 0, piece, 0, 0)
        )
        in_specs.append(pl.BlockSpec((step, rows, cols), lambda b, h: (b, 0, 0)))
        args.append(received)
        if into is not None:
            in_specs.append(pl.BlockSpec(memory_space=pl.ANY))
            aliases = {len(args): 0}
            args.append(into)
    return pl.pallas_call(
        outer_kernel,
        grid_spec=pltpu.PrefetchScalarGridSpec(
            num_scalar_prefetch=1, grid=(size // step,), in_specs=in_specs, out_specs=out_spec
        ),
        out_shape=jax.ShapeDtypeStruct(shape, jnp.bfloat16),
        input_output_aliases=aliases,
        compiler_params=pltpu.CompilerParams(vmem_limit_bytes=VMEM),
        cost_estimate=pl.CostEstimate(
            flops=2 * size * rows * cols * channels,
            bytes_accessed=2 * size * (rows * cols + rows * channels + cols * channels),
            transcendentals=0,
        ),
    )(*args)


def back_kernel(groups, factor_ref, slope_ref, *refs):
    *rows_refs, out_ref = refs
    blocks, depth, width = factor_ref.shape
    share = depth // groups // len(rows_refs)
    for n in range(blocks):
        factor = factor_ref[n].reshape(groups, len(rows_refs), share, width)
        total = sum(
            lax.dot_general(
                factor[:, piece].reshape(groups * share, width),
                rows_ref[n],
                (((0,), (0,)), ((), ())),
                preferred_element_type=jnp.float32,
            )
            for piece, rows_ref in enumerate(rows_refs)
        )
        at = pl.ds(n * width, width)
        out_ref[at] = (total * slope_ref[at]).astype(jnp.bfloat16)


def back(factor, pieces, slope, groups):
    blocks, depth, width = factor.shape
    channels = slope.shape[1]
    step = 2 if blocks % 2 == 0 else 1
    return pl.pallas_call(
        functools.partial(back_kernel, groups),
        grid=(blocks // step,),
        in_specs=[
            pl.BlockSpec((step, depth, width), lambda b: (b, 0, 0)),
            pl.BlockSpec((step * width, channels), lambda b: (b, 0)),
        ]
        + [pl.BlockSpec((step, *rows.shape[1:]), lambda b: (b, 0, 0)) for rows in pieces],
        out_specs=pl.BlockSpec((step * width, channels), lambda b: (b, 0)),
        out_shape=jax.ShapeDtypeStruct((blocks * width, channels), jnp.bfloat16),
        compiler_params=pltpu.CompilerParams(vmem_limit_bytes=VMEM),
        cost_estimate=pl.CostEstimate(
            flops=2 * blocks * depth * width * channels,
            bytes_accessed=2 * blocks * (depth * width + depth * channels + 3 * width * channels),
            transcendentals=0,
        ),
    )(factor, slope, *pieces)


def gate_kernel(taps, rows_ref, before_ref, previous_ref, weight_ref, hidden_ref, slope_ref):
    rows = rows_ref[...].astype(jnp.float32)

    def write(before):
        extended = jnp.concatenate([before[...].astype(jnp.float32), rows], axis=0)
        conv = weight_ref[0:1, :] * rows
        for r in range(1, taps):
            conv += weight_ref[r : r + 1, :] * pltpu.roll(extended, r, 0)[before.shape[0] :]
        gate = jax.nn.sigmoid(conv)
        hidden_ref[...] = (conv * gate).astype(jnp.bfloat16)
        slope_ref[...] = gate * (1.0 + conv * (1.0 - gate))

    @pl.when(pl.program_id(0) == 0)
    def _():
        write(previous_ref)

    @pl.when(pl.program_id(0) > 0)
    def _():
        write(before_ref)


def gated(signal, previous, conv_weight, rows):
    tokens, channels = signal.shape
    previous = jnp.pad(previous, ((ROW_TILE - previous.shape[0], 0), (0, 0)))
    step = rows // ROW_TILE
    whole = pl.BlockSpec((rows, channels), lambda b: (b, 0))
    return pl.pallas_call(
        functools.partial(gate_kernel, conv_weight.shape[0]),
        grid=(tokens // rows,),
        in_specs=[
            whole,
            pl.BlockSpec((ROW_TILE, channels), lambda b: (jnp.maximum(b * step - 1, 0), 0)),
            pl.BlockSpec((ROW_TILE, channels), lambda b: (0, 0)),
            pl.BlockSpec(conv_weight.shape, lambda b: (0, 0)),
        ],
        out_specs=[whole, whole],
        out_shape=[
            jax.ShapeDtypeStruct((tokens, channels), jnp.bfloat16),
            jax.ShapeDtypeStruct((tokens, channels), jnp.float32),
        ],
        compiler_params=pltpu.CompilerParams(vmem_limit_bytes=VMEM),
        cost_estimate=pl.CostEstimate(
            flops=20 * tokens * channels, bytes_accessed=8 * tokens * channels, transcendentals=tokens * channels
        ),
    )(signal, signal, previous, conv_weight)


def signal_kernel(cuts_, taps, *refs):
    pieces, firsts = refs[: len(cuts_)], refs[len(cuts_) : 2 * len(cuts_)]
    following_ref, weight_ref, out_ref = refs[2 * len(cuts_) :]
    block, last = pl.program_id(0), pl.num_programs(0) - 1

    def spread(rows, next_rows):
        rows = rows[...].astype(jnp.float32)
        extended = jnp.concatenate([rows, next_rows[...].astype(jnp.float32)], axis=0)
        total = weight_ref[0:1, :] * rows
        for r in range(1, taps):
            ahead = pltpu.roll(extended, extended.shape[0] - r, 0)[: rows.shape[0]]
            total += weight_ref[r : r + 1, :] * ahead
        out_ref[...] = total.astype(jnp.bfloat16)

    for n, (start, size) in enumerate(cuts_):
        end = start + size - 1

        @pl.when((block >= start) & (block < end))
        def _():
            spread(pieces[n], firsts[n])

        @pl.when(block == end)
        def _():
            spread(pieces[n], following_ref if n == len(cuts_) - 1 else firsts[n + 1])


def signal_back(grad_conv, following, conv_weight, cuts_, rows):
    channels = conv_weight.shape[1]
    blocks = sum(size for _, size in cuts_)
    following = jnp.pad(following, ((0, ROW_TILE - following.shape[0]), (0, 0)))
    step = rows // ROW_TILE

    def own(start, size):
        return lambda b: (jnp.clip(b - start, 0, size - 1), 0)

    def first_rows(start, size):
        return lambda b: (jnp.clip(b + 1 - start, 0, size - 1) * step, 0)

    return pl.pallas_call(
        functools.partial(signal_kernel, cuts_, conv_weight.shape[0]),
        grid=(blocks,),
        in_specs=[pl.BlockSpec((rows, channels), own(*cut)) for cut in cuts_]
        + [pl.BlockSpec((ROW_TILE, channels), first_rows(*cut)) for cut in cuts_]
        + [
            pl.BlockSpec((ROW_TILE, channels), lambda b: (0, 0)),
            pl.BlockSpec(conv_weight.shape, lambda b: (0, 0)),
        ],
        out_specs=pl.BlockSpec((rows, channels), lambda b: (b, 0)),
        out_shape=jax.ShapeDtypeStruct((blocks * rows, channels), jnp.bfloat16),
        compiler_params=pltpu.CompilerParams(vmem_limit_bytes=VMEM),
        cost_estimate=pl.CostEstimate(
            flops=WEIGHT * 8 * blocks * rows * channels,
            bytes_accessed=WEIGHT * 4 * blocks * rows * channels,
            transcendentals=0,
        ),
    )(*grad_conv, *grad_conv, following, conv_weight)


def body(signal, conv_weight, first_factor, second_factor, grad_output):
    _, tok_rows, channels = signal.shape
    blocks, block_order = first_factor.shape[0], first_factor.shape[1]
    col_blocks, block_count = second_factor.shape[0], second_factor.shape[1]
    tap_count = conv_weight.shape[0]
    devices = lax.axis_size("seq")
    mine = lax.axis_index("batch")[None]
    theirs = 1 - mine
    tail = tap_count - 1

    first_cuts = cuts(col_blocks, (16, 16))
    second_cuts = cuts(col_blocks, (12, 9, 6, 5))
    second_late = (0, 1, 0, 0) if len(second_cuts) > 1 else (0,)
    first_shares = (8, 22, 2) if len(second_cuts) > 1 else (blocks,)
    tied = lax.optimization_barrier

    def swapped(part):
        return lax.ppermute(part, "batch", [(0, 1), (1, 0)])

    def exchanged(sent):
        return lax.all_to_all(sent, "seq", 0, 0, tiled=True)

    def ordered(rows):
        return rows.reshape(-1, blocks, channels).transpose(1, 0, 2)

    previous = passed_along(signal[0, tok_rows - tail :, :], "seq", 1)
    upstream = grad_output.reshape(col_blocks, block_count, channels)
    sent = split_product(second_factor, upstream, devices, *first_cuts[0])
    sent, previous = tied((sent, previous))

    arrived = exchanged(sent)
    hidden, slope = gated(signal[0], previous, conv_weight, block_order)
    later, hidden = tied((upstream, hidden))
    rest = [split_product(second_factor, later, devices, *cut) for cut in first_cuts[1:]]
    hidden = hidden.reshape(blocks, block_order, channels)
    mixed = jnp.einsum(
        "ikj,ijd->ikd", first_factor, hidden, preferred_element_type=jnp.float32
    ).astype(jnp.bfloat16)
    by_owner = mixed.reshape(blocks, devices, col_blocks, channels).transpose(1, 2, 0, 3)
    pieces = [by_owner[:, start : start + size] for start, size in second_cuts]
    arrived, hidden, slope, *rest = tied((arrived, hidden, slope, *pieces, *rest))
    pieces, rest = rest[: len(pieces)], rest[len(pieces) :]

    shape_first = (blocks, devices // lax.axis_size("batch"), len(first_cuts))
    row_pieces, got_first, grad_first = [], [], None
    for sent in rest:
        coming = exchanged(sent)
        rows = ordered(arrived)
        got = swapped(outer(theirs, rows, hidden, size=blocks))
        arrived, rows, got, hidden, *pieces = tied((coming, rows, got, hidden, *pieces))
        row_pieces.append(rows)
        got_first.append(got)

    columns = exchanged(pieces[0])
    rows = ordered(arrived)
    row_pieces.append(rows)
    shares = cuts(blocks, first_shares)
    parts = [outer(theirs, rows, hidden, start, start, size) for start, size in shares]
    last = min(1, len(parts) - 1)
    rows, parts[last] = tied((rows, parts[last]))
    got_shares = [swapped(parts[0])]
    if last:
        parts[last], got_shares[0] = tied((parts[last], got_shares[0]))
        got_shares.append(swapped(parts[last]))
    late_first = parts[2:]
    grad_conv = back(first_factor, [*row_pieces[:-1], rows], slope, devices)
    following = passed_along(grad_conv[:tail, :], "seq", -1)
    for piece, earlier in enumerate(got_first):
        grad_first = outer(
            mine, row_pieces[piece], hidden, size=blocks, target=(earlier, grad_first, shape_first, 0, piece)
        )
    state = [columns, following, got_shares[-1], grad_conv, *pieces[1:], *late_first]
    if got_first:
        state.append(grad_first)
    state = list(tied(tuple(state)))
    if got_first:
        grad_first = state.pop()
    late_first = [state.pop() for _ in late_first]
    columns, following, got_shares[-1], grad_conv, *pieces = state

    def own_first(start, size, got):
        return lambda into: outer(
            mine,
            row_pieces[-1],
            hidden,
            start,
            start,
            size,
            target=(got, into, shape_first, start, len(first_cuts) - 1),
        )

    def own_second(start, at, size, columns):
        return lambda got: lambda into: outer(
            mine, upstream, columns, start, at, size, target=(got, into, shape_second, start, 0)
        )

    shape_second = (col_blocks, 1, 1)
    grad_second = grad_signal = None
    adding_first = [own_first(*share, got) for share, got in zip(shares, got_shares)]
    adding_second = []
    held = [(late_first[0], None)] if late_first else []
    for step, (start, size) in enumerate(second_cuts):
        coming = exchanged(pieces[step]) if pieces[step:] else None
        early = size - second_late[step]
        part = outer(theirs, upstream, columns, start, 0, early)
        late_part = None
        if second_late[step]:
            late_part = outer(theirs, upstream, columns, start + early, early, second_late[step])
        got_late = finish = None
        if held:
            got_late, finish = swapped(held[0][0]), held[0][1]
            part, got_late = tied((part, got_late))
        got = swapped(part)
        if step == 0:
            grad_signal = signal_back([grad_conv], following, conv_weight, [(0, blocks)], block_order)
        for add in adding_first:
            grad_first = add(grad_first)
        for add in adding_second:
            grad_second = add(grad_second)
        adding_first, adding_second = [], []
        now = [got, grad_signal, grad_first]
        now += [value for value in (got_late, late_part, grad_second) if value is not None]
        if coming is not None:
            tied_now = list(tied((coming, *now, *pieces[step + 1 :])))
            following_columns, got, grad_signal, grad_first, *rest = tied_now
            if got_late is not None:
                got_late = rest.pop(0)
            if late_part is not None:
                late_part = rest.pop(0)
            if grad_second is not None:
                grad_second = rest.pop(0)
            pieces[step + 1 :] = rest
        if got_late is not None:
            if finish is None:
                adding_first.append(own_first(*shares[-1], got_late))
            else:
                adding_second.append(finish(got_late))
        adding_second.append(own_second(start, 0, early, columns)(got))
        held = []
        if late_part is not None:
            held = [(late_part, own_second(start + early, early, second_late[step], columns))]
        if coming is not None:
            columns = following_columns
    for add in adding_first:
        grad_first = add(grad_first)
    for add in adding_second:
        grad_second = add(grad_second)
    grad_first = grad_first.reshape(blocks, -1, block_order)
    grad_second = grad_second.reshape(col_blocks, -1, block_count)
    return (
        grad_signal[None],
        grad_first,
        grad_second,
    )


def solution(mesh):
    placed = (
        P("batch", "seq", None),
        P(),
        P("seq", None, None),
        P("seq", None, None),
        P("batch", "seq", None),
    )
    return jax.shard_map(
        body,
        mesh=mesh,
        in_specs=placed,
        out_specs=(P("batch", "seq", None), P("seq", "batch", None), P("seq", "batch", None)),
        check_vma=False,
    )
```

```python
import functools

import jax
import jax.numpy as jnp
from jax import lax
from jax.experimental import pallas as pl
from jax.experimental.pallas import tpu as pltpu
from jax.sharding import PartitionSpec as P

ROW_TILE = 16
VMEM = 64 * 2**20 - 2**18
WEIGHT = 1


def passed_along(value, axis, steps):
    count = lax.axis_size(axis)
    initial, last = (max(0, -steps), min(count, count - steps))
    return lax.ppermute(value, axis, [(source, source + steps) for source in range(initial, last)])


def cuts(total, sizes):
    if sum(sizes) != total:
        sizes = (total,)
    return [(sum(sizes[:n]), size) for n, size in enumerate(sizes)]


def per_step(blocks, start=0):
    return next(n for n in (4, 2, 1) if blocks % n == 0 and start % n == 0)


def split_product_kernel(factor_ref, rows_ref, out_ref):
    devices = out_ref.shape[0]
    for n in range(factor_ref.shape[0]):
        product = lax.dot_general(
            factor_ref[n], rows_ref[n], (((0,), (0,)), ((), ())), preferred_element_type=jnp.float32
        ).astype(jnp.bfloat16)
        out_ref[:, n] = product.reshape(devices, product.shape[0] // devices, product.shape[1])


def split_product(factor, rows, devices, start, size):
    _, depth, width = factor.shape
    channels = rows.shape[2]
    part = width // devices
    if part % ROW_TILE:
        product = jnp.einsum(
            "kmi,kmd->kid",
            factor[start : start + size],
            rows[start : start + size],
            preferred_element_type=jnp.float32,
        ).astype(jnp.bfloat16)
        return product.reshape(size, devices, part, channels).transpose(1, 0, 2, 3)
    step = per_step(size, start)
    at = start // step
    return pl.pallas_call(
        split_product_kernel,
        grid=(size // step,),
        in_specs=[
            pl.BlockSpec((step, depth, width), lambda k: (k + at, 0, 0)),
            pl.BlockSpec((step, depth, channels), lambda k: (k + at, 0, 0)),
        ],
        out_specs=pl.BlockSpec((devices, step, part, channels), lambda k: (0, k, 0, 0)),
        out_shape=jax.ShapeDtypeStruct((devices, size, part, channels), jnp.bfloat16),
        compiler_params=pltpu.CompilerParams(vmem_limit_bytes=VMEM),
        cost_estimate=pl.CostEstimate(
            flops=2 * size * depth * width * channels,
            bytes_accessed=2 * size * (depth * width + depth * channels + width * channels),
            transcendentals=0,
        ),
    )(factor, rows)


def outer_kernel(half_ref, left_ref, right_ref, *refs):
    out_ref = refs[-1]
    channels = left_ref.shape[-1]
    for n in range(left_ref.shape[0]):
        right = right_ref[n] if len(right_ref.shape) == 3 else right_ref[:, n].reshape(-1, channels)
        product = lax.dot_general(
            left_ref[n], right, (((1,), (1,)), ((), ())), preferred_element_type=jnp.float32
        ).astype(jnp.bfloat16)
        if len(refs) == 1:
            out_ref[n] = product
        else:
            total = product.astype(jnp.float32) + refs[0][n].astype(jnp.float32)
            _, groups, _, rows, cols = out_ref.shape
            out_ref[n, :, 0] = total.astype(jnp.bfloat16).reshape(groups, rows, cols)


def outer(half, left, right, left_start=0, right_start=0, size=None, target=None):
    halves = lax.axis_size("batch")
    rows, channels = left.shape[1] // halves, left.shape[2]
    if right.ndim == 4 and right.shape[2] % ROW_TILE:
        right = right.transpose(1, 0, 2, 3).reshape(right.shape[1], -1, channels)
    out_start = target[3] if target else 0
    step = next(n for n in (4, 5, 2, 1) if not any(v % n for v in (size, right_start, out_start)))
    right_at, out_at = right_start // step, out_start // step
    if right.ndim == 4:
        devices, _, part, _ = right.shape
        cols = devices * part
        right_spec = pl.BlockSpec((devices, step, part, channels), lambda b, h: (0, b + right_at, 0, 0))
    else:
        cols = right.shape[1]
        right_spec = pl.BlockSpec((step, cols, channels), lambda b, h: (b + right_at, 0, 0))
    left_block = tuple(pl.Element(n) for n in (step, rows, channels))
    left_spec = pl.BlockSpec(left_block, lambda b, h: (b * step + left_start, pl.multiple_of(h[0] * rows, rows), 0))
    in_specs = [left_spec, right_spec]
    args, aliases = [half, left, right], {}
    if target is None:
        shape, out_spec = (size, rows, cols), pl.BlockSpec((step, rows, cols), lambda b, h: (b, 0, 0))
    else:
        received, into, (blocks, groups, pieces), _, piece = target
        shape = (blocks, groups, pieces, rows // groups, cols)
        out_spec = pl.BlockSpec(
            (step, groups, 1, rows // groups, cols), lambda b, h: (b + out_at, 0, piece, 0, 0)
        )
        in_specs.append(pl.BlockSpec((step, rows, cols), lambda b, h: (b, 0, 0)))
        args.append(received)
        if into is not None:
            in_specs.append(pl.BlockSpec(memory_space=pl.ANY))
            aliases = {len(args): 0}
            args.append(into)
    return pl.pallas_call(
        outer_kernel,
        grid_spec=pltpu.PrefetchScalarGridSpec(
            num_scalar_prefetch=1, grid=(size // step,), in_specs=in_specs, out_specs=out_spec
        ),
        out_shape=jax.ShapeDtypeStruct(shape, jnp.bfloat16),
        input_output_aliases=aliases,
        compiler_params=pltpu.CompilerParams(vmem_limit_bytes=VMEM),
        cost_estimate=pl.CostEstimate(
            flops=2 * size * rows * cols * channels,
            bytes_accessed=2 * size * (rows * cols + rows * channels + cols * channels),
            transcendentals=0,
        ),
    )(*args)


def back_kernel(groups, factor_ref, slope_ref, *refs):
    *rows_refs, out_ref = refs
    blocks, depth, width = factor_ref.shape
    share = depth // groups // len(rows_refs)
    for n in range(blocks):
        factor = factor_ref[n].reshape(groups, len(rows_refs), share, width)
        total = sum(
            lax.dot_general(
                factor[:, piece].reshape(groups * share, width),
                rows_ref[n],
                (((0,), (0,)), ((), ())),
                preferred_element_type=jnp.float32,
            )
            for piece, rows_ref in enumerate(rows_refs)
        )
        at = pl.ds(n * width, width)
        out_ref[at] = (total * slope_ref[at]).astype(jnp.bfloat16)


def back(factor, pieces, slope, groups):
    blocks, depth, width = factor.shape
    channels = slope.shape[1]
    step = 2 if blocks % 2 == 0 else 1
    return pl.pallas_call(
        functools.partial(back_kernel, groups),
        grid=(blocks // step,),
        in_specs=[
            pl.BlockSpec((step, depth, width), lambda b: (b, 0, 0)),
            pl.BlockSpec((step * width, channels), lambda b: (b, 0)),
        ]
        + [pl.BlockSpec((step, *rows.shape[1:]), lambda b: (b, 0, 0)) for rows in pieces],
        out_specs=pl.BlockSpec((step * width, channels), lambda b: (b, 0)),
        out_shape=jax.ShapeDtypeStruct((blocks * width, channels), jnp.bfloat16),
        compiler_params=pltpu.CompilerParams(vmem_limit_bytes=VMEM),
        cost_estimate=pl.CostEstimate(
            flops=2 * blocks * depth * width * channels,
            bytes_accessed=2 * blocks * (depth * width + depth * channels + 3 * width * channels),
            transcendentals=0,
        ),
    )(factor, slope, *pieces)


def gate_kernel(taps, rows_ref, before_ref, previous_ref, weight_ref, hidden_ref, slope_ref):
    rows = rows_ref[...].astype(jnp.float32)

    def write(before):
        extended = jnp.concatenate([before[...].astype(jnp.float32), rows], axis=0)
        conv = weight_ref[0:1, :] * rows
        for r in range(1, taps):
            conv += weight_ref[r : r + 1, :] * pltpu.roll(extended, r, 0)[before.shape[0] :]
        gate = jax.nn.sigmoid(conv)
        hidden_ref[...] = (conv * gate).astype(jnp.bfloat16)
        slope_ref[...] = gate * (1.0 + conv * (1.0 - gate))

    @pl.when(pl.program_id(0) == 0)
    def _():
        write(previous_ref)

    @pl.when(pl.program_id(0) > 0)
    def _():
        write(before_ref)


def gated(signal, previous, conv_weight, rows):
    tokens, channels = signal.shape
    previous = jnp.pad(previous, ((ROW_TILE - previous.shape[0], 0), (0, 0)))
    step = rows // ROW_TILE
    whole = pl.BlockSpec((rows, channels), lambda b: (b, 0))
    return pl.pallas_call(
        functools.partial(gate_kernel, conv_weight.shape[0]),
        grid=(tokens // rows,),
        in_specs=[
            whole,
            pl.BlockSpec((ROW_TILE, channels), lambda b: (jnp.maximum(b * step - 1, 0), 0)),
            pl.BlockSpec((ROW_TILE, channels), lambda b: (0, 0)),
            pl.BlockSpec(conv_weight.shape, lambda b: (0, 0)),
        ],
        out_specs=[whole, whole],
        out_shape=[
            jax.ShapeDtypeStruct((tokens, channels), jnp.bfloat16),
            jax.ShapeDtypeStruct((tokens, channels), jnp.float32),
        ],
        compiler_params=pltpu.CompilerParams(vmem_limit_bytes=VMEM),
        cost_estimate=pl.CostEstimate(
            flops=20 * tokens * channels, bytes_accessed=8 * tokens * channels, transcendentals=tokens * channels
        ),
    )(signal, signal, previous, conv_weight)


def signal_kernel(cuts_, taps, *refs):
    pieces, firsts = refs[: len(cuts_)], refs[len(cuts_) : 2 * len(cuts_)]
    following_ref, weight_ref, out_ref = refs[2 * len(cuts_) :]
    block, last = pl.program_id(0), pl.num_programs(0) - 1

    def spread(rows, next_rows):
        rows = rows[...].astype(jnp.float32)
        extended = jnp.concatenate([rows, next_rows[...].astype(jnp.float32)], axis=0)
        total = weight_ref[0:1, :] * rows
        for r in range(1, taps):
            ahead = pltpu.roll(extended, extended.shape[0] - r, 0)[: rows.shape[0]]
            total += weight_ref[r : r + 1, :] * ahead
        out_ref[...] = total.astype(jnp.bfloat16)

    for n, (start, size) in enumerate(cuts_):
        end = start + size - 1

        @pl.when((block >= start) & (block < end))
        def _():
            spread(pieces[n], firsts[n])

        @pl.when(block == end)
        def _():
            spread(pieces[n], following_ref if n == len(cuts_) - 1 else firsts[n + 1])


def signal_back(grad_conv, following, conv_weight, cuts_, rows):
    channels = conv_weight.shape[1]
    blocks = sum(size for _, size in cuts_)
    following = jnp.pad(following, ((0, ROW_TILE - following.shape[0]), (0, 0)))
    step = rows // ROW_TILE

    def own(start, size):
        return lambda b: (jnp.clip(b - start, 0, size - 1), 0)

    def first_rows(start, size):
        return lambda b: (jnp.clip(b + 1 - start, 0, size - 1) * step, 0)

    return pl.pallas_call(
        functools.partial(signal_kernel, cuts_, conv_weight.shape[0]),
        grid=(blocks,),
        in_specs=[pl.BlockSpec((rows, channels), own(*cut)) for cut in cuts_]
        + [pl.BlockSpec((ROW_TILE, channels), first_rows(*cut)) for cut in cuts_]
        + [
            pl.BlockSpec((ROW_TILE, channels), lambda b: (0, 0)),
            pl.BlockSpec(conv_weight.shape, lambda b: (0, 0)),
        ],
        out_specs=pl.BlockSpec((rows, channels), lambda b: (b, 0)),
        out_shape=jax.ShapeDtypeStruct((blocks * rows, channels), jnp.bfloat16),
        compiler_params=pltpu.CompilerParams(vmem_limit_bytes=VMEM),
        cost_estimate=pl.CostEstimate(
            flops=WEIGHT * 8 * blocks * rows * channels,
            bytes_accessed=WEIGHT * 4 * blocks * rows * channels,
            transcendentals=0,
        ),
    )(*grad_conv, *grad_conv, following, conv_weight)


def body(signal, conv_weight, first_factor, second_factor, grad_output):
    _, tok_rows, channels = signal.shape
    blocks, block_order = first_factor.shape[0], first_factor.shape[1]
    col_blocks, block_count = second_factor.shape[0], second_factor.shape[1]
    tap_count = conv_weight.shape[0]
    devices = lax.axis_size("seq")
    mine = lax.axis_index("batch")[None]
    theirs = 1 - mine
    tail = tap_count - 1

    first_cuts = cuts(col_blocks, (16, 16))
    second_cuts = cuts(col_blocks, (12, 9, 6, 5))
    second_late = (0, 1, 0, 0) if len(second_cuts) > 1 else (0,)
    first_shares = (8, 22, 2) if len(second_cuts) > 1 else (blocks,)
    tied = lax.optimization_barrier

    def swapped(part):
        return lax.ppermute(part, "batch", [(0, 1), (1, 0)])

    def exchanged(sent):
        return lax.all_to_all(sent, "seq", 0, 0, tiled=True)

    def ordered(rows):
        return rows.reshape(-1, blocks, channels).transpose(1, 0, 2)

    previous = passed_along(signal[0, tok_rows - tail :, :], "seq", 1)
    upstream = grad_output.reshape(col_blocks, block_count, channels)
    sent = split_product(second_factor, upstream, devices, *first_cuts[0])
    sent, previous = tied((sent, previous))

    arrived = exchanged(sent)
    hidden, slope = gated(signal[0], previous, conv_weight, block_order)
    later, hidden = tied((upstream, hidden))
    rest = [split_product(second_factor, later, devices, *cut) for cut in first_cuts[1:]]
    hidden = hidden.reshape(blocks, block_order, channels)
    mixed = jnp.einsum(
        "ikj,ijd->ikd", first_factor, hidden, preferred_element_type=jnp.float32
    ).astype(jnp.bfloat16)
    by_owner = mixed.reshape(blocks, devices, col_blocks, channels).transpose(1, 2, 0, 3)
    pieces = [by_owner[:, start : start + size] for start, size in second_cuts]
    arrived, hidden, slope, *rest = tied((arrived, hidden, slope, *pieces, *rest))
    pieces, rest = rest[: len(pieces)], rest[len(pieces) :]

    shape_first = (blocks, devices // lax.axis_size("batch"), len(first_cuts))
    row_pieces, got_first, grad_first = [], [], None
    for sent in rest:
        coming = exchanged(sent)
        rows = ordered(arrived)
        got = swapped(outer(theirs, rows, hidden, size=blocks))
        arrived, rows, got, hidden, *pieces = tied((coming, rows, got, hidden, *pieces))
        row_pieces.append(rows)
        got_first.append(got)

    columns = exchanged(pieces[0])
    rows = ordered(arrived)
    row_pieces.append(rows)
    shares = cuts(blocks, first_shares)
    parts = [outer(theirs, rows, hidden, start, start, size) for start, size in shares]
    last = min(1, len(parts) - 1)
    rows, parts[last] = tied((rows, parts[last]))
    got_shares = [swapped(parts[0])]
    if last:
        parts[last], got_shares[0] = tied((parts[last], got_shares[0]))
        got_shares.append(swapped(parts[last]))
    late_first = parts[2:]
    grad_conv = back(first_factor, [*row_pieces[:-1], rows], slope, devices)
    following = passed_along(grad_conv[:tail, :], "seq", -1)
    for piece, earlier in enumerate(got_first):
        grad_first = outer(
            mine, row_pieces[piece], hidden, size=blocks, target=(earlier, grad_first, shape_first, 0, piece)
        )
    state = [columns, following, got_shares[-1], grad_conv, *pieces[1:], *late_first]
    if got_first:
        state.append(grad_first)
    state = list(tied(tuple(state)))
    if got_first:
        grad_first = state.pop()
    late_first = [state.pop() for _ in late_first]
    columns, following, got_shares[-1], grad_conv, *pieces = state

    def own_first(start, size, got):
        return lambda into: outer(
            mine,
            row_pieces[-1],
            hidden,
            start,
            start,
            size,
            target=(got, into, shape_first, start, len(first_cuts) - 1),
        )

    def own_second(start, at, size, columns):
        return lambda got: lambda into: outer(
            mine, upstream, columns, start, at, size, target=(got, into, shape_second, start, 0)
        )

    shape_second = (col_blocks, 1, 1)
    grad_second = grad_signal = None
    adding_first = [own_first(*share, got) for share, got in zip(shares, got_shares)]
    adding_second = []
    held = [(late_first[0], None)] if late_first else []
    for step, (start, size) in enumerate(second_cuts):
        coming = exchanged(pieces[step]) if pieces[step:] else None
        early = size - second_late[step]
        split = 3 if coming is None and early == 5 else 0
        part = outer(theirs, upstream, columns, start, 0, split or early)
        late_part = None
        if second_late[step]:
            late_part = outer(theirs, upstream, columns, start + early, early, second_late[step])
        got_late = finish = None
        if held:
            got_late, finish = swapped(held[0][0]), held[0][1]
            part, got_late = tied((part, got_late))
        got = swapped(part)
        if split:
            final = swapped(outer(theirs, upstream, columns, start + split, split, early - split))
        if step == 0:
            grad_signal = signal_back([grad_conv], following, conv_weight, [(0, blocks)], block_order)
        for add in adding_first:
            grad_first = add(grad_first)
        for add in adding_second:
            grad_second = add(grad_second)
        adding_first, adding_second = [], []
        now = [got, grad_signal, grad_first]
        now += [value for value in (got_late, late_part, grad_second) if value is not None]
        if coming is not None:
            tied_now = list(tied((coming, *now, *pieces[step + 1 :])))
            following_columns, got, grad_signal, grad_first, *rest = tied_now
            if got_late is not None:
                got_late = rest.pop(0)
            if late_part is not None:
                late_part = rest.pop(0)
            if grad_second is not None:
                grad_second = rest.pop(0)
            pieces[step + 1 :] = rest
        if got_late is not None:
            if finish is None:
                adding_first.append(own_first(*shares[-1], got_late))
            else:
                adding_second.append(finish(got_late))
        adding_second.append(own_second(start, 0, split or early, columns)(got))
        if split:
            adding_second.append(own_second(start + split, split, early - split, columns)(final))
        held = []
        if late_part is not None:
            held = [(late_part, own_second(start + early, early, second_late[step], columns))]
        if coming is not None:
            columns = following_columns
    for add in adding_first:
        grad_first = add(grad_first)
    for add in adding_second:
        grad_second = add(grad_second)
    grad_first = grad_first.reshape(blocks, -1, block_order)
    grad_second = grad_second.reshape(col_blocks, -1, block_count)
    return (
        grad_signal[None],
        grad_first,
        grad_second,
    )


def solution(mesh):
    placed = (
        P("batch", "seq", None),
        P(),
        P("seq", None, None),
        P("seq", None, None),
        P("batch", "seq", None),
    )
    return jax.shard_map(
        body,
        mesh=mesh,
        in_specs=placed,
        out_specs=(P("batch", "seq", None), P("seq", "batch", None), P("seq", "batch", None)),
        check_vma=False,
    )
```
